32 devices in a mesh: groups: 2 (over y), frame: 4 (over z), head: 2 (over x), sub: 2 (over core).
Axes of the slice: x: 2, y: 2, z: 4, core: 2. Of those that a mesh axis runs over, the one named last changes fastest.
Arguments:
- queries: bfloat16 [3072, 2560], P(('groups', 'frame'), ('head', 'sub')), parts along dimension 0, may hold values from -6 to 6, as said below
- keyvals: bfloat16 [2, 3072, 2560], P(None, ('groups', 'frame'), ('head', 'sub')), parts along dimension 1, may hold values from -6 to 6, as said below
- residual_in: float32 [3072, 5120], P(('groups', 'frame'), ('head', 'sub')), parts along dimension 0, may hold values from -3 to 3
- gate: float32 [10240], P(('groups', 'head', 'sub')), parts along dimension 0, may hold values from -4 to 4
- out_weight: bfloat16 [2560, 5120], P(('head', 'sub'), 'frame'), may hold values from -0.125 to 0.125
- pattern: int32 [48, 8], P(('groups', 'frame')), parts along dimension 0, may hold values from 0 to 23, as said below
- live: int32 [48], P(('groups', 'frame')), parts along dimension 0, may hold values from 4 to 8
Outputs:
- updated: float32 [3072, 5120], P(('groups', 'frame'), ('head', 'sub')), parts along dimension 0
The draws below stay inside these ranges and needn't reach their ends.
There are 2 independent parts, one for each index of `groups`. The reference program is written for one: setup_inputs(seed, part) draws one part's arguments, and reference() takes and returns one part's arrays. A program takes and returns all parts, laid end to end along the dimension named above; an argument that names none is the same for every part. Nothing has to cross between parts.
Inputs may be any that keep to these rules, and one draw needn't show every extreme that they name: `pattern`: entry 0 of each row is the query tile itself; entries below live of that row are distinct tiles lying in the query tile's frame or one frame before or after it; later entries repeat the query tile. `queries`: values of order one. `keyvals`: values of order one.
All inputs are finite; a program needn't handle non-finite values.
Results may differ from the reference program's by a relative error of at most 0.0065.
Values may be sent and summed in bfloat16 or wider, within the bound.
A program may use at most 128 MiB of HBM per device.

```python
import math
import jax
import jax.numpy as jnp
from jax import lax

D = 5120
HEAD_DIM = 128
HEAD_DEV = 5
TILE = 64
TILES_F = 6
KSEL = 8
HEADS = 20
FRAMES = 4
TOKENS = 1536
N_HEAD = 2
N_SUB = 2


def base_field(key, salt):
    shape = (FRAMES * TILES_F * TILE, HEADS * HEAD_DIM)
    field = jnp.clip(jax.random.normal(jax.random.fold_in(key, salt), shape, jnp.float32), -5.0, 5.0)
    return field


def draw_queries(key, part):
    field = base_field(key, 21)
    return field.astype(jnp.bfloat16)


def draw_keyvals(key, part):
    keys = base_field(key, 22)
    values = base_field(key, 23)
    return jnp.stack([keys, values]).astype(jnp.bfloat16)


def tile_lists(key):
    tiles = FRAMES * TILES_F
    width = 3 * TILES_F
    own = jnp.arange(tiles, dtype=jnp.int32)
    own_frame = own // TILES_F
    own_spot = own % TILES_F
    column = jnp.arange(width, dtype=jnp.int32)
    cand_frame = own_frame[:, None] + column[None, :] // TILES_F - 1
    cand_spot = jnp.broadcast_to(column[None, :] % TILES_F, (tiles, width))
    valid = (cand_frame >= 0) & (cand_frame < FRAMES)
    is_self = (cand_frame == own_frame[:, None]) & (cand_spot == own_spot[:, None])
    noise = jax.random.randint(jax.random.fold_in(key, 31), (tiles, width), 0, 1 << 20)
    score = jnp.where(is_self, 1 << 29, jnp.where(valid, noise * width + column[None, :] + width, column[None, :] + 0 * noise))
    ranked, order = lax.top_k(score, KSEL)
    cand_id = cand_frame * TILES_F + cand_spot
    picked = jnp.take_along_axis(cand_id, order, axis=1)
    count = jnp.sum(valid.astype(jnp.int32), axis=1)
    wanted = jax.random.randint(jax.random.fold_in(key, 32), (tiles,), KSEL // 2, KSEL + 1)
    used = jnp.minimum(wanted, count)
    forced = jax.random.randint(jax.random.fold_in(key, 33), (), TILES_F, tiles - TILES_F)
    used = jnp.where(own == forced, KSEL, used)
    slot = jnp.arange(KSEL, dtype=jnp.int32)
    lists = jnp.where(slot[None, :] < used[:, None], picked, own[:, None])
    return (lists.astype(jnp.int32), used.astype(jnp.int32))


def draw_pattern(key, part):
    lists, used = tile_lists(key)
    return lists


def draw_live(key, part):
    lists, used = tile_lists(key)
    return used


def block_scale(key, dims, cuts, least, top_value):
    level = 1.0
    for dim, shards_of in cuts:
        draws = jax.random.uniform(jax.random.fold_in(jax.random.fold_in(key, 6), dim), (shards_of,), jnp.float32, least / len(cuts), top_value / len(cuts))
        level = level * jnp.repeat(jnp.exp(draws), dims[dim] // shards_of).reshape((-1,) + (1,) * (len(dims) - 1 - dim))
    return level


def bell_draw(key, shape, scale, bound, shards=(), kind=jnp.bfloat16):
    drawn = scale * jax.random.normal(key, shape, jnp.float32)
    if shards:
        drawn = drawn * block_scale(key, shape, shards, -0.22, 0.18)
    return jnp.clip(drawn, -bound, bound).astype(kind)


def setup_inputs(seed: int = 0, part: int = 0) -> dict:
    splits = jax.random.split(jax.random.key(seed), 8)
    own_keys = jax.random.split(jax.random.fold_in(splits[7], part), 8)
    queries = draw_queries(jax.random.fold_in(jax.random.fold_in(splits[7], part), 71), part)
    keyvals = draw_keyvals(jax.random.fold_in(jax.random.fold_in(splits[7], part), 71), part)
    residual_in = bell_draw(own_keys[2], (TOKENS, D), 0.5, 3.0, ((0, 4), (1, 4)), jnp.float32)
    gate = bell_draw(own_keys[3], (D,), 1.0, 4.0, ((0, 4),), jnp.float32)
    out_weight = bell_draw(splits[4], (HEADS * HEAD_DIM, D), (HEADS * HEAD_DIM) ** -0.5, 0.125, ((0, 4), (1, 4)))
    pattern = draw_pattern(jax.random.fold_in(jax.random.fold_in(splits[7], part), 71), part)
    live = draw_live(jax.random.fold_in(jax.random.fold_in(splits[7], part), 71), part)
    return {"queries": queries, "keyvals": keyvals, "residual_in": residual_in, "gate": gate, "out_weight": out_weight, "pattern": pattern, "live": live}


def attend_tile(tile_queries, key_rows, value_rows, count):
    scores = jnp.einsum('qhd,khd->hqk', tile_queries.astype(jnp.float32), key_rows.astype(jnp.float32)) * (1.0 / math.sqrt(HEAD_DIM))
    slot = jnp.arange(KSEL * TILE, dtype=jnp.int32) // TILE
    scores = jnp.where((slot < count)[None, None, :], scores, -1e+30)
    row_max = lax.optimization_barrier(jnp.max(scores, axis=-1, keepdims=True))
    expo = jnp.exp(scores - row_max)
    probs = (expo / lax.optimization_barrier(jnp.sum(expo, axis=-1, keepdims=True))).astype(jnp.bfloat16)
    return jnp.einsum('hqk,khd->qhd', probs.astype(jnp.float32), value_rows.astype(jnp.float32)).astype(jnp.bfloat16)

def reference(queries, keyvals, residual_in, gate, out_weight, pattern, live):
    tiles = FRAMES * TILES_F
    query_tiles = queries.reshape(tiles, TILE, HEADS, HEAD_DIM)
    key_tiles = keyvals[0].reshape(tiles, TILE, HEADS, HEAD_DIM)
    value_tiles = keyvals[1].reshape(tiles, TILE, HEADS, HEAD_DIM)

    def one_tile(packed):
        tile_queries, listed, count = packed
        key_rows = key_tiles[listed].reshape(KSEL * TILE, HEADS, HEAD_DIM)
        value_rows = value_tiles[listed].reshape(KSEL * TILE, HEADS, HEAD_DIM)
        return attend_tile(tile_queries, key_rows, value_rows, count)
    attended = lax.map(one_tile, (query_tiles, pattern, live))
    attended = attended.reshape(tiles * TILE, HEADS * HEAD_DIM)
    group_width = HEAD_DEV * HEAD_DIM

    def add_group(total, group):
        start = (group * group_width).astype(jnp.int32)
        columns = lax.dynamic_slice_in_dim(attended, start, group_width, 1)
        weights = lax.dynamic_slice_in_dim(out_weight, start, group_width, 0)
        term = jnp.dot(columns, weights, preferred_element_type=jnp.float32).astype(jnp.bfloat16)
        term = lax.optimization_barrier(term)
        return (total + term.astype(jnp.float32), None)
    empty = jnp.zeros((tiles * TILE, D), jnp.float32)
    projected, _ = lax.scan(add_group, empty, jnp.arange(N_HEAD * N_SUB, dtype=jnp.int32))
    return residual_in + gate[None, :] * projected
```

```python
import functools
import math

import jax
import jax.numpy as jnp
from jax import lax
from jax.experimental import pallas as pl
from jax.experimental.pallas import tpu as pltpu
from jax.sharding import PartitionSpec as P

HEAD_DIM = 128
TILES_F = 6
KSEL = 8
COLS = 256
VMEM_LIMIT = 48 * 1024 * 1024
MESH = pl.DeviceIdType.MESH


def padded_2(block, axis, dim, width):
    count = lax.axis_size(axis)
    forward = [(i, i + 1) for i in range(count - 1)]
    backward = [(target, source) for source, target in forward]
    low = lax.ppermute(
        lax.slice_in_dim(block, block.shape[dim] - width, None, axis=dim), axis, forward
    )
    high = lax.ppermute(lax.slice_in_dim(block, 0, width, axis=dim), axis, backward)
    return jnp.concatenate([low, block, high], axis=dim)


def attend(first_tile, pattern_ref, live_ref, q_ref, kv_ref, att_ref):
    tile_count, tile_rows, width = q_ref.shape
    held = kv_ref.shape[1]
    scale = 1.0 / math.sqrt(HEAD_DIM)
    slot = lax.broadcasted_iota(jnp.int32, (tile_rows, KSEL * tile_rows), 1) // tile_rows

    def one_tile(t, carry):
        ids = [jnp.clip(pattern_ref[t, s] - first_tile, 0, held - 1) for s in range(KSEL)]
        keys = jnp.concatenate([kv_ref[0, i] for i in ids], axis=0)
        values = jnp.concatenate([kv_ref[1, i] for i in ids], axis=0)
        tile_queries = q_ref[t]
        allowed = slot < live_ref[t]
        for h in range(width // HEAD_DIM):
            cols = slice(h * HEAD_DIM, (h + 1) * HEAD_DIM)
            scores = lax.dot_general(
                tile_queries[:, cols],
                keys[:, cols],
                (((1,), (1,)), ((), ())),
                preferred_element_type=jnp.float32,
            )
            scores = jnp.where(allowed, scores * scale, -1e30)
            expo = jnp.exp(scores - jnp.max(scores, axis=-1, keepdims=True))
            probs = expo * (1.0 / jnp.sum(expo, axis=-1, keepdims=True))
            out = jnp.dot(
                probs.astype(jnp.bfloat16), values[:, cols], preferred_element_type=jnp.float32
            )
            rows = pl.ds(pl.multiple_of(t * tile_rows, tile_rows), tile_rows)
            att_ref[rows, cols] = out.astype(jnp.bfloat16)
        return carry

    lax.fori_loop(0, tile_count, one_tile, 0)


def attend_kernel(first_ref, pattern_ref, live_ref, q_ref, kv_ref, att_ref):
    attend(first_ref[0], pattern_ref, live_ref, q_ref, kv_ref, att_ref)


def plain_sum(queries, keyvals, out_weight, pattern, live):
    rows, width = queries.shape
    tile_count = pattern.shape[0]
    tile_rows = rows // tile_count
    padded = padded_2(keyvals, "frame", 1, TILES_F * tile_rows)
    first_tile = lax.axis_index("frame") * tile_count - TILES_F
    smem = pl.BlockSpec(memory_space=pltpu.SMEM)
    vmem = pl.BlockSpec(memory_space=pltpu.VMEM)
    attended = pl.pallas_call(
        attend_kernel,
        out_shape=jax.ShapeDtypeStruct((rows, width), jnp.bfloat16),
        in_specs=[smem, smem, smem, vmem, vmem],
        out_specs=vmem,
        compiler_params=pltpu.CompilerParams(vmem_limit_bytes=VMEM_LIMIT),
    )(
        jnp.reshape(first_tile, (1,)).astype(jnp.int32),
        pattern,
        live,
        queries.reshape(tile_count, tile_rows, width),
        padded.reshape(2, -1, tile_rows, width),
    )
    partial_rows = jnp.dot(
        attended,
        lax.all_gather(out_weight, "frame", axis=1, tiled=True),
        preferred_element_type=jnp.float32,
    )
    return lax.psum_scatter(
        partial_rows.astype(jnp.bfloat16), ("head", "sub"), scatter_dimension=1, tiled=True
    ).astype(jnp.float32)


def fused_kernel(
    frames, pattern_ref, live_ref, q_ref, kv_ref, w_ref, out_ref,
    kvbuf, wbuf, att, tmp, coresend, corebuf, xsend, xbuf,
    own_sem, halo_send, halo_recv, right_send, left_send, w_recv, y_send, y_recv,
    core_send, core_recv, x_send, x_recv,
):
    g, f = lax.axis_index("groups"), lax.axis_index("frame")
    x, core = lax.axis_index("head"), lax.axis_index("sub")
    tiles = q_ref.shape[0]
    depth, span = w_ref.shape
    half = depth // 2
    last = frames - 1
    to_left, to_right = {"frame": f - 1}, {"frame": f + 1}
    to_y, to_core, to_x = {"groups": 1 - g}, {"sub": 1 - core}, {"head": 1 - x}
    mine = pl.ds(pl.multiple_of(g * half, half), half)
    other = pl.ds(pl.multiple_of((1 - g) * half, half), half)

    barrier = pltpu.get_barrier_semaphore()

    def greet(where):
        pl.semaphore_signal(barrier, inc=1, device_id=where, device_id_type=MESH)

    for where in (to_y, to_core, to_x):
        greet(where)
    pl.when(f > 0)(lambda: greet(to_left))
    pl.when(f < last)(lambda: greet(to_right))
    ends = jnp.where(f > 0, 1, 0) + jnp.where(f < last, 1, 0)
    pl.semaphore_wait(barrier, 3 + ends)

    def remote(src, dst, send, recv, where):
        return pltpu.make_async_remote_copy(
            src_ref=src, dst_ref=dst, send_sem=send, recv_sem=recv,
            device_id=where, device_id_type=MESH,
        )

    own = pltpu.make_async_copy(kv_ref, kvbuf.at[:, pl.ds(tiles, tiles)], own_sem)
    low, high = kvbuf.at[:, pl.ds(0, tiles)], kvbuf.at[:, pl.ds(2 * tiles, tiles)]
    halo_right = remote(kv_ref, low, halo_send.at[0], halo_recv.at[0], to_right)
    halo_left = remote(kv_ref, high, halo_send.at[1], halo_recv.at[1], to_left)

    def along(chunk, where, sems, first=False):
        piece = wbuf.at[chunk, mine]
        return remote(
            w_ref.at[mine] if first else piece, piece, sems.at[chunk], w_recv.at[chunk], where
        )

    def across(chunk):
        piece = wbuf.at[chunk, mine]
        return remote(piece, piece, y_send.at[chunk], y_recv.at[chunk], to_y)

    pl.when(f < last)(halo_right.start)
    pl.when(f > 0)(halo_left.start)
    pl.when(f < last)(along(f, to_right, right_send, True).start)
    pl.when(f > 0)(along(f, to_left, left_send, True).start)
    own.start()

    def arrive(distance):
        @pl.when(f >= distance)
        def _():
            chunk = f - distance
            along(chunk, to_right, right_send).wait_recv()
            pl.when(f < last)(along(chunk, to_right, right_send).start)
            across(chunk).start()

        @pl.when(f + distance <= last)
        def _():
            chunk = f + distance
            along(chunk, to_left, left_send).wait_recv()
            pl.when(f > 0)(along(chunk, to_left, left_send).start)
            across(chunk).start()

    own.wait()
    pl.when(f > 0)(halo_right.wait_recv)
    pl.when(f < last)(halo_left.wait_recv)
    arrive(1)
    attend(f * tiles - tiles, pattern_ref, live_ref, q_ref, kvbuf, att)

    def core_copy(slot):
        return remote(
            coresend.at[slot], corebuf.at[slot], core_send.at[slot], core_recv.at[slot], to_core
        )

    x_copy = remote(xsend, xbuf, x_send, x_recv, to_x)

    def each_tile(body):
        @pl.loop(0, span // COLS)
        def _(n):
            body(pl.ds(pl.multiple_of(n * COLS, COLS), COLS))

    def project(chunk, weights):
        slot, parity = chunk // 2, chunk % 2

        def term(cols):
            tmp[:, cols] = jnp.dot(
                att[...], weights[:, cols], preferred_element_type=jnp.float32
            )

        each_tile(term)

        @pl.when(parity != core)
        def _():
            def pack(cols):
                coresend[slot, :, cols] = tmp[:, cols].astype(jnp.bfloat16)

            each_tile(pack)
            core_copy(slot).start()

        @pl.when(parity == core)
        def _():
            core_copy(slot).wait_recv()

            @pl.when(slot == x)
            def _():
                def keep(cols):
                    out_ref[:, cols] = tmp[:, cols] + corebuf[slot, :, cols].astype(jnp.float32)

                each_tile(keep)

            @pl.when(slot != x)
            def _():
                def pack(cols):
                    both = tmp[:, cols] + corebuf[slot, :, cols].astype(jnp.float32)
                    xsend[:, cols] = both.astype(jnp.bfloat16)

                each_tile(pack)
                x_copy.start()

    def step(chunk):
        piece = wbuf.at[chunk, other]
        remote(piece, piece, y_send.at[chunk], y_recv.at[chunk], to_y).wait_recv()
        project(chunk, wbuf.at[chunk])

    project(f, w_ref)
    for distance in range(1, frames):
        if distance + 1 < frames:
            arrive(distance + 1)
        pl.when(f >= distance)(lambda: step(f - distance))
        pl.when(f + distance <= last)(lambda: step(f + distance))

    x_copy.wait_recv()

    def finish(cols):
        out_ref[:, cols] = out_ref[:, cols] + xbuf[:, cols].astype(jnp.float32)

    each_tile(finish)

    x_copy.wait_send()
    for slot in range(2):
        core_copy(slot).wait_send()
    pl.when(f < last)(halo_right.wait_send)
    pl.when(f > 0)(halo_left.wait_send)
    pl.when(f < last)(along(f, to_right, right_send, True).wait_send)
    pl.when(f > 0)(along(f, to_left, left_send, True).wait_send)
    for distance in range(1, frames):

        @pl.when(f >= distance)
        def _():
            chunk = f - distance
            pl.when(f < last)(along(chunk, to_right, right_send).wait_send)
            across(chunk).wait_send()

        @pl.when(f + distance <= last)
        def _():
            chunk = f + distance
            pl.when(f > 0)(along(chunk, to_left, left_send).wait_send)
            across(chunk).wait_send()


def fused_sum(queries, keyvals, out_weight, pattern, live):
    rows, width = queries.shape
    frames = lax.axis_size("frame")
    tiles = pattern.shape[0]
    tile_rows = rows // tiles
    depth, span = out_weight.shape
    smem = pl.BlockSpec(memory_space=pltpu.SMEM)
    vmem = pl.BlockSpec(memory_space=pltpu.VMEM)
    dma = pltpu.SemaphoreType.DMA
    return pl.pallas_call(
        functools.partial(fused_kernel, frames),
        out_shape=jax.ShapeDtypeStruct((rows, span), jnp.float32),
        in_specs=[smem, smem, vmem, vmem, vmem],
        out_specs=vmem,
        scratch_shapes=[
            pltpu.VMEM((2, 3 * tiles, tile_rows, width), jnp.bfloat16),
            pltpu.VMEM((frames, depth, span), jnp.bfloat16),
            pltpu.VMEM((rows, width), jnp.bfloat16),
            pltpu.VMEM((rows, span), jnp.float32),
            pltpu.VMEM((2, rows, span), jnp.bfloat16),
            pltpu.VMEM((2, rows, span), jnp.bfloat16),
            pltpu.VMEM((rows, span), jnp.bfloat16),
            pltpu.VMEM((rows, span), jnp.bfloat16),
            dma(()), dma((2,)), dma((2,)), dma((frames,)), dma((frames,)), dma((frames,)),
            dma((frames,)), dma((frames,)), dma((2,)), dma((2,)), dma(()), dma(()),
        ],
        compiler_params=pltpu.CompilerParams(
            collective_id=0, has_side_effects=True, vmem_limit_bytes=VMEM_LIMIT
        ),
        cost_estimate=pl.CostEstimate(
            flops=2 * rows * depth * span * frames, bytes_accessed=8 << 20, transcendentals=1 << 20
        ),
    )(
        pattern,
        live,
        queries.reshape(tiles, tile_rows, width),
        keyvals.reshape(2, tiles, tile_rows, width),
        out_weight,
    )


def per_device(queries, keyvals, residual_in, gate, out_weight, pattern, live):
    size = lax.axis_size
    fits = (
        size("groups") == size("head") == size("sub") == 2
        and size("frame") == 4
        and pattern.shape[0] == TILES_F
        and out_weight.shape[0] % 32 == 0
        and out_weight.shape[1] % COLS == 0
    )
    total = fused_sum if fits else plain_sum
    return residual_in + gate[None, :] * total(queries, keyvals, out_weight, pattern, live)


def solution(mesh):
    in_specs = (
        P(("groups", "frame"), ("head", "sub")),
        P(None, ("groups", "frame"), ("head", "sub")),
        P(("groups", "frame"), ("head", "sub")),
        P(("groups", "head", "sub")),
        P(("head", "sub"), "frame"),
        P(("groups", "frame"), None),
        P(("groups", "frame")),
    )
    out_specs = P(("groups", "frame"), ("head", "sub"))
    return jax.shard_map(
        per_device, mesh=mesh, in_specs=in_specs, out_specs=out_specs, check_vma=False
    )
```

```python
import functools
import math

import jax
import jax.numpy as jnp
from jax import lax
from jax.experimental import pallas as pl
from jax.experimental.pallas import tpu as pltpu
from jax.sharding import PartitionSpec as P

HEAD_DIM = 128
TILES_F = 6
KSEL = 8
COLS = 256
VMEM_LIMIT = 48 * 1024 * 1024
FUSED_LIMIT = 60 * 1024 * 1024
MESH = pl.DeviceIdType.MESH


def padded_2(block, axis, dim, width):
    count = lax.axis_size(axis)
    forward = [(i, i + 1) for i in range(count - 1)]
    backward = [(target, source) for source, target in forward]
    low = lax.ppermute(
        lax.slice_in_dim(block, block.shape[dim] - width, None, axis=dim), axis, forward
    )
    high = lax.ppermute(lax.slice_in_dim(block, 0, width, axis=dim), axis, backward)
    return jnp.concatenate([low, block, high], axis=dim)


def attend(first_tile, pattern_ref, live_ref, q_ref, kv_ref, att_ref, between=None):
    tile_count, tile_rows, width = q_ref.shape
    held = kv_ref.shape[1]
    scale = 1.0 / math.sqrt(HEAD_DIM)
    slot = lax.broadcasted_iota(jnp.int32, (tile_rows, KSEL * tile_rows), 1) // tile_rows

    def one_tile(t, carry):
        ids = [jnp.clip(pattern_ref[t, s] - first_tile, 0, held - 1) for s in range(KSEL)]
        keys = jnp.concatenate([kv_ref[0, i] for i in ids], axis=0)
        values = jnp.concatenate([kv_ref[1, i] for i in ids], axis=0)
        tile_queries = q_ref[t]
        allowed = slot < live_ref[t]
        for h in range(width // HEAD_DIM):
            cols = slice(h * HEAD_DIM, (h + 1) * HEAD_DIM)
            scores = lax.dot_general(
                tile_queries[:, cols],
                keys[:, cols],
                (((1,), (1,)), ((), ())),
                preferred_element_type=jnp.float32,
            )
            scores = jnp.where(allowed, scores * scale, -1e30)
            expo = jnp.exp(scores - jnp.max(scores, axis=-1, keepdims=True))
            probs = expo * (1.0 / jnp.sum(expo, axis=-1, keepdims=True))
            out = jnp.dot(
                probs.astype(jnp.bfloat16), values[:, cols], preferred_element_type=jnp.float32
            )
            rows = pl.ds(pl.multiple_of(t * tile_rows, tile_rows), tile_rows)
            att_ref[rows, cols] = out.astype(jnp.bfloat16)
        if between is not None:
            between(t)
        return carry

    lax.fori_loop(0, tile_count, one_tile, 0)


def attend_kernel(first_ref, pattern_ref, live_ref, q_ref, kv_ref, att_ref):
    attend(first_ref[0], pattern_ref, live_ref, q_ref, kv_ref, att_ref)


def plain_sum(queries, keyvals, out_weight, pattern, live):
    rows, width = queries.shape
    tile_count = pattern.shape[0]
    tile_rows = rows // tile_count
    padded = padded_2(keyvals, "frame", 1, TILES_F * tile_rows)
    first_tile = lax.axis_index("frame") * tile_count - TILES_F
    smem = pl.BlockSpec(memory_space=pltpu.SMEM)
    vmem = pl.BlockSpec(memory_space=pltpu.VMEM)
    attended = pl.pallas_call(
        attend_kernel,
        out_shape=jax.ShapeDtypeStruct((rows, width), jnp.bfloat16),
        in_specs=[smem, smem, smem, vmem, vmem],
        out_specs=vmem,
        compiler_params=pltpu.CompilerParams(vmem_limit_bytes=VMEM_LIMIT),
    )(
        jnp.reshape(first_tile, (1,)).astype(jnp.int32),
        pattern,
        live,
        queries.reshape(tile_count, tile_rows, width),
        padded.reshape(2, -1, tile_rows, width),
    )
    partial_rows = jnp.dot(
        attended,
        lax.all_gather(out_weight, "frame", axis=1, tiled=True),
        preferred_element_type=jnp.float32,
    )
    return lax.psum_scatter(
        partial_rows.astype(jnp.bfloat16), ("head", "sub"), scatter_dimension=1, tiled=True
    ).astype(jnp.float32)


def fused_kernel(
    frames, pattern_ref, live_ref, q_hbm, kv_hbm, w_hbm, out_ref,
    q_ref, kvbuf, w_ref, wbuf, att, coresend, corebuf, xsend, xbuf,
    own_sem, halo_send, halo_recv, right_send, left_send, w_recv, y_send, y_recv,
    core_send, core_recv, x_send, x_recv,
):
    g, f = lax.axis_index("groups"), lax.axis_index("frame")
    x, core = lax.axis_index("head"), lax.axis_index("sub")
    tiles = q_ref.shape[0]
    depth, span = w_ref.shape
    pieces = span // COLS
    half = depth // 2
    last = frames - 1
    to_left, to_right = {"frame": f - 1}, {"frame": f + 1}
    to_y, to_core, to_x = {"groups": 1 - g}, {"sub": 1 - core}, {"head": 1 - x}
    mine = pl.ds(pl.multiple_of(g * half, half), half)
    other = pl.ds(pl.multiple_of((1 - g) * half, half), half)

    own = [
        pltpu.make_async_copy(kv_hbm, kvbuf.at[:, pl.ds(tiles, tiles)], own_sem.at[0]),
        pltpu.make_async_copy(q_hbm, q_ref, own_sem.at[1]),
        pltpu.make_async_copy(w_hbm, w_ref, own_sem.at[2]),
    ]
    for copy in own:
        copy.start()

    barrier = pltpu.get_barrier_semaphore()

    def greet(where):
        pl.semaphore_signal(barrier, inc=1, device_id=where, device_id_type=MESH)

    for where in (to_y, to_core, to_x):
        greet(where)
    pl.when(f > 0)(lambda: greet(to_left))
    pl.when(f < last)(lambda: greet(to_right))
    ends = jnp.where(f > 0, 1, 0) + jnp.where(f < last, 1, 0)
    pl.semaphore_wait(barrier, 3 + ends)

    def remote(src, dst, send, recv, where):
        return pltpu.make_async_remote_copy(
            src_ref=src, dst_ref=dst, send_sem=send, recv_sem=recv,
            device_id=where, device_id_type=MESH,
        )

    def columns(j):
        return pl.ds(pl.multiple_of(j * COLS, COLS), COLS)

    low, high = kvbuf.at[:, pl.ds(0, tiles)], kvbuf.at[:, pl.ds(2 * tiles, tiles)]
    halo_right = remote(kv_hbm, low, halo_send.at[0], halo_recv.at[0], to_right)
    halo_left = remote(kv_hbm, high, halo_send.at[1], halo_recv.at[1], to_left)

    def along(chunk, j, where, sems, first=False):
        piece = wbuf.at[chunk, mine, columns(j)]
        src = w_hbm.at[mine, columns(j)] if first else piece
        return remote(src, piece, sems.at[chunk, j], w_recv.at[chunk, j], where)

    def across(chunk, j, rows):
        piece = wbuf.at[chunk, rows, columns(j)]
        return remote(piece, piece, y_send.at[chunk, j], y_recv.at[chunk, j], to_y)

    def each_piece(body, start=0):
        def run(j, carry):
            body(j)
            return carry

        lax.fori_loop(start, pieces, run, 0)

    def launch(j):
        pl.when(f < last)(along(f, j, to_right, right_send, True).start)
        pl.when(f > 0)(along(f, j, to_left, left_send, True).start)

    def arrive(distance, j):
        @pl.when(f >= distance)
        def _():
            chunk = f - distance
            along(chunk, j, to_right, right_send).wait_recv()
            pl.when(f < last)(along(chunk, j, to_right, right_send).start)
            across(chunk, j, mine).start()

        @pl.when(f + distance <= last)
        def _():
            chunk = f + distance
            along(chunk, j, to_left, left_send).wait_recv()
            pl.when(f > 0)(along(chunk, j, to_left, left_send).start)
            across(chunk, j, mine).start()

    pl.when(f < last)(halo_right.start)
    pl.when(f > 0)(halo_left.start)
    launch(0)
    for copy in own:
        copy.wait()
    pl.when(f > 0)(halo_right.wait_recv)
    pl.when(f < last)(halo_left.wait_recv)
    each_piece(launch, 1)

    def between(t):
        pl.when(t < pieces)(lambda: arrive(1, t))

    attend(f * tiles - tiles, pattern_ref, live_ref, q_ref, kvbuf, att, between)

    def core_copy(slot, j):
        return remote(
            coresend.at[slot, :, columns(j)], corebuf.at[slot, :, columns(j)],
            core_send.at[slot, j], core_recv.at[slot, j], to_core,
        )

    def x_copy(j):
        return remote(
            xsend.at[:, columns(j)], xbuf.at[:, columns(j)], x_send.at[j], x_recv.at[j], to_x
        )

    def project(chunk, j, weights):
        slot, parity = chunk // 2, chunk % 2
        cols = columns(j)
        term = jnp.dot(att[...], weights[:, cols], preferred_element_type=jnp.float32)

        @pl.when(parity != core)
        def _():
            coresend[slot, :, cols] = term.astype(jnp.bfloat16)
            core_copy(slot, j).start()

        @pl.when(parity == core)
        def _():
            out_or_send = slot == x
            core_copy(slot, j).wait_recv()
            both = term + corebuf[slot, :, cols].astype(jnp.float32)

            @pl.when(out_or_send)
            def _():
                out_ref[:, cols] = both

            @pl.when(jnp.logical_not(out_or_send))
            def _():
                xsend[:, cols] = both.astype(jnp.bfloat16)
                x_copy(j).start()

    def step(distance, j):
        def one(chunk):
            across(chunk, j, other).wait_recv()
            project(chunk, j, wbuf.at[chunk])

        pl.when(f >= distance)(lambda: one(f - distance))
        pl.when(f + distance <= last)(lambda: one(f + distance))

    each_piece(lambda j: project(f, j, w_ref))
    for distance in range(1, last):

        def events(j):
            arrive(distance + 1, j)
            step(distance, j)
            if distance + 1 == last:
                pl.when(j >= 2)(lambda: step(last, j - 2))

        each_piece(events)
    each_piece(lambda j: step(last, j), pieces - 2)

    def finish(j):
        x_copy(j).wait_recv()
        cols = columns(j)
        out_ref[:, cols] = out_ref[:, cols] + xbuf[:, cols].astype(jnp.float32)

    each_piece(finish)

    pl.when(f < last)(halo_right.wait_send)
    pl.when(f > 0)(halo_left.wait_send)

    def drain(j):
        x_copy(j).wait_send()
        for slot in range(2):
            core_copy(slot, j).wait_send()
        pl.when(f < last)(along(f, j, to_right, right_send, True).wait_send)
        pl.when(f > 0)(along(f, j, to_left, left_send, True).wait_send)
        for distance in range(1, frames):

            @pl.when(f >= distance)
            def _():
                chunk = f - distance
                pl.when(f < last)(along(chunk, j, to_right, right_send).wait_send)
                across(chunk, j, mine).wait_send()

            @pl.when(f + distance <= last)
            def _():
                chunk = f + distance
                pl.when(f > 0)(along(chunk, j, to_left, left_send).wait_send)
                across(chunk, j, mine).wait_send()

    each_piece(drain)


def fused_sum(queries, keyvals, out_weight, pattern, live):
    rows, width = queries.shape
    frames = lax.axis_size("frame")
    tiles = pattern.shape[0]
    tile_rows = rows // tiles
    depth, span = out_weight.shape
    pieces = span // COLS
    smem = pl.BlockSpec(memory_space=pltpu.SMEM)
    vmem = pl.BlockSpec(memory_space=pltpu.VMEM)
    anywhere = pl.BlockSpec(memory_space=pl.ANY)
    dma = pltpu.SemaphoreType.DMA
    bf16 = jnp.bfloat16
    return pl.pallas_call(
        functools.partial(fused_kernel, frames),
        out_shape=jax.ShapeDtypeStruct((rows, span), jnp.float32),
        in_specs=[smem, smem, anywhere, anywhere, anywhere],
        out_specs=vmem,
        scratch_shapes=[
            pltpu.VMEM((tiles, tile_rows, width), bf16),
            pltpu.VMEM((2, 3 * tiles, tile_rows, width), bf16),
            pltpu.VMEM((depth, span), bf16),
            pltpu.VMEM((frames, depth, span), bf16),
            pltpu.VMEM((rows, width), bf16),
            pltpu.VMEM((2, rows, span), bf16),
            pltpu.VMEM((2, rows, span), bf16),
            pltpu.VMEM((rows, span), bf16),
            pltpu.VMEM((rows, span), bf16),
            dma((3,)), dma((2,)), dma((2,)),
            dma((frames, pieces)), dma((frames, pieces)), dma((frames, pieces)),
            dma((frames, pieces)), dma((frames, pieces)),
            dma((2, pieces)), dma((2, pieces)), dma((pieces,)), dma((pieces,)),
        ],
        compiler_params=pltpu.CompilerParams(
            collective_id=0, has_side_effects=True, vmem_limit_bytes=FUSED_LIMIT
        ),
        cost_estimate=pl.CostEstimate(
            flops=2 * rows * depth * span * frames, bytes_accessed=8 << 20, transcendentals=1 << 20
        ),
    )(
        pattern,
        live,
        queries.reshape(tiles, tile_rows, width),
        keyvals.reshape(2, tiles, tile_rows, width),
        out_weight,
    )


def per_device(queries, keyvals, residual_in, gate, out_weight, pattern, live):
    size = lax.axis_size
    fits = (
        size("groups") == size("head") == size("sub") == 2
        and size("frame") == 4
        and pattern.shape[0] == TILES_F
        and out_weight.shape[1] <= TILES_F * COLS
        and out_weight.shape[0] % 32 == 0
        and out_weight.shape[1] % COLS == 0
    )
    total = fused_sum if fits else plain_sum
    return residual_in + gate[None, :] * total(queries, keyvals, out_weight, pattern, live)


def solution(mesh):
    in_specs = (
        P(("groups", "frame"), ("head", "sub")),
        P(None, ("groups", "frame"), ("head", "sub")),
        P(("groups", "frame"), ("head", "sub")),
        P(("groups", "head", "sub")),
        P(("head", "sub"), "frame"),
        P(("groups", "frame"), None),
        P(("groups", "frame")),
    )
    out_specs = P(("groups", "frame"), ("head", "sub"))
    return jax.shard_map(
        per_device, mesh=mesh, in_specs=in_specs, out_specs=out_specs, check_vma=False
    )
```

```python
import functools
import math

import jax
import jax.numpy as jnp
from jax import lax
from jax.experimental import pallas as pl
from jax.experimental.pallas import tpu as pltpu
from jax.sharding import PartitionSpec as P

HEAD_DIM = 128
TILES_F = 6
KSEL = 8
COLS = 256
VMEM_LIMIT = 48 * 1024 * 1024
FUSED_LIMIT = 60 * 1024 * 1024
MESH = pl.DeviceIdType.MESH


def padded_2(block, axis, dim, width):
    count = lax.axis_size(axis)
    forward = [(i, i + 1) for i in range(count - 1)]
    backward = [(target, source) for source, target in forward]
    low = lax.ppermute(
        lax.slice_in_dim(block, block.shape[dim] - width, None, axis=dim), axis, forward
    )
    high = lax.ppermute(lax.slice_in_dim(block, 0, width, axis=dim), axis, backward)
    return jnp.concatenate([low, block, high], axis=dim)


def attend(first_tile, pattern_ref, live_ref, q_ref, kv_ref, att_ref, between=None):
    tile_count, tile_rows, width = q_ref.shape
    held = kv_ref.shape[1]
    scale = 1.0 / math.sqrt(HEAD_DIM)
    slot = lax.broadcasted_iota(jnp.int32, (tile_rows, KSEL * tile_rows), 1) // tile_rows

    def one_tile(t, carry):
        ids = [jnp.clip(pattern_ref[t, s] - first_tile, 0, held - 1) for s in range(KSEL)]
        keys = jnp.concatenate([kv_ref[0, i] for i in ids], axis=0)
        values = jnp.concatenate([kv_ref[1, i] for i in ids], axis=0)
        tile_queries = q_ref[t]
        allowed = slot < live_ref[t]
        for h in range(width // HEAD_DIM):
            cols = slice(h * HEAD_DIM, (h + 1) * HEAD_DIM)
            scores = lax.dot_general(
                tile_queries[:, cols],
                keys[:, cols],
                (((1,), (1,)), ((), ())),
                preferred_element_type=jnp.float32,
            )
            scores = jnp.where(allowed, scores * scale, -1e30)
            expo = jnp.exp(scores - jnp.max(scores, axis=-1, keepdims=True))
            probs = expo * (1.0 / jnp.sum(expo, axis=-1, keepdims=True))
            out = jnp.dot(
                probs.astype(jnp.bfloat16), values[:, cols], preferred_element_type=jnp.float32
            )
            rows = pl.ds(pl.multiple_of(t * tile_rows, tile_rows), tile_rows)
            att_ref[rows, cols] = out.astype(jnp.bfloat16)
        if between is not None:
            between(t)
        return carry

    lax.fori_loop(0, tile_count, one_tile, 0)


def attend_kernel(first_ref, pattern_ref, live_ref, q_ref, kv_ref, att_ref):
    attend(first_ref[0], pattern_ref, live_ref, q_ref, kv_ref, att_ref)


def plain_sum(queries, keyvals, out_weight, pattern, live):
    rows, width = queries.shape
    tile_count = pattern.shape[0]
    tile_rows = rows // tile_count
    padded = padded_2(keyvals, "frame", 1, TILES_F * tile_rows)
    first_tile = lax.axis_index("frame") * tile_count - TILES_F
    smem = pl.BlockSpec(memory_space=pltpu.SMEM)
    vmem = pl.BlockSpec(memory_space=pltpu.VMEM)
    attended = pl.pallas_call(
        attend_kernel,
        out_shape=jax.ShapeDtypeStruct((rows, width), jnp.bfloat16),
        in_specs=[smem, smem, smem, vmem, vmem],
        out_specs=vmem,
        compiler_params=pltpu.CompilerParams(vmem_limit_bytes=VMEM_LIMIT),
    )(
        jnp.reshape(first_tile, (1,)).astype(jnp.int32),
        pattern,
        live,
        queries.reshape(tile_count, tile_rows, width),
        padded.reshape(2, -1, tile_rows, width),
    )
    partial_rows = jnp.dot(
        attended,
        lax.all_gather(out_weight, "frame", axis=1, tiled=True),
        preferred_element_type=jnp.float32,
    )
    return lax.psum_scatter(
        partial_rows.astype(jnp.bfloat16), ("head", "sub"), scatter_dimension=1, tiled=True
    ).astype(jnp.float32)


def fused_kernel(
    frames, pattern_ref, live_ref, q_hbm, kv_hbm, w_hbm, out_ref,
    q_ref, kvbuf, w_ref, wbuf, att, coresend, corebuf, xsend, xbuf,
    own_sem, halo_send, halo_recv, right_send, left_send, w_recv, y_send, y_recv,
    core_send, core_recv, x_send, x_recv,
):
    g, f = lax.axis_index("groups"), lax.axis_index("frame")
    x, core = lax.axis_index("head"), lax.axis_index("sub")
    tiles = q_ref.shape[0]
    depth, span = w_ref.shape
    pieces = span // COLS
    half = depth // 2
    last = frames - 1
    to_left, to_right = {"frame": f - 1}, {"frame": f + 1}
    to_y, to_core, to_x = {"groups": 1 - g}, {"sub": 1 - core}, {"head": 1 - x}
    mine = pl.ds(pl.multiple_of(g * half, half), half)
    other = pl.ds(pl.multiple_of((1 - g) * half, half), half)

    own = [
        pltpu.make_async_copy(kv_hbm, kvbuf.at[:, pl.ds(tiles, tiles)], own_sem.at[0]),
        pltpu.make_async_copy(q_hbm, q_ref, own_sem.at[1]),
        pltpu.make_async_copy(w_hbm, w_ref, own_sem.at[2]),
    ]
    for copy in own:
        copy.start()

    barrier = pltpu.get_barrier_semaphore()

    def greet(where):
        pl.semaphore_signal(barrier, inc=1, device_id=where, device_id_type=MESH)

    for where in (to_y, to_core, to_x):
        greet(where)
    pl.when(f > 0)(lambda: greet(to_left))
    pl.when(f < last)(lambda: greet(to_right))
    ends = jnp.where(f > 0, 1, 0) + jnp.where(f < last, 1, 0)
    pl.semaphore_wait(barrier, 3 + ends)

    def remote(src, dst, send, recv, where):
        return pltpu.make_async_remote_copy(
            src_ref=src, dst_ref=dst, send_sem=send, recv_sem=recv,
            device_id=where, device_id_type=MESH,
        )

    def columns(j):
        return pl.ds(pl.multiple_of(j * COLS, COLS), COLS)

    low, high = kvbuf.at[:, pl.ds(0, tiles)], kvbuf.at[:, pl.ds(2 * tiles, tiles)]
    halo_right = remote(kv_hbm, low, halo_send.at[0], halo_recv.at[0], to_right)
    halo_left = remote(kv_hbm, high, halo_send.at[1], halo_recv.at[1], to_left)

    def along(chunk, j, where, sems, first=False):
        piece = wbuf.at[chunk, mine, columns(j)]
        src = w_hbm.at[mine, columns(j)] if first else piece
        return remote(src, piece, sems.at[chunk, j], w_recv.at[chunk, j], where)

    def across(chunk, j, rows):
        piece = wbuf.at[chunk, rows, columns(j)]
        return remote(piece, piece, y_send.at[chunk, j], y_recv.at[chunk, j], to_y)

    def each_piece(body, start=0):
        def run(j, carry):
            body(j)
            return carry

        lax.fori_loop(start, pieces, run, 0)

    def launch(j):
        pl.when(f < last)(along(f, j, to_right, right_send, True).start)
        pl.when(f > 0)(along(f, j, to_left, left_send, True).start)

    def take(distance, j):
        @pl.when(f >= distance)
        def _():
            along(f - distance, j, to_right, right_send).wait_recv()
            across(f - distance, j, mine).start()

        @pl.when(f + distance <= last)
        def _():
            along(f + distance, j, to_left, left_send).wait_recv()
            across(f + distance, j, mine).start()

    def pass_on(distance, j):
        rightward = jnp.logical_and(f >= distance, f < last)
        leftward = jnp.logical_and(f + distance <= last, f > 0)
        pl.when(rightward)(along(f - distance, j, to_right, right_send).start)
        pl.when(leftward)(along(f + distance, j, to_left, left_send).start)

    def arrive(distance, j):
        take(distance, j)
        pass_on(distance, j)

    each_piece(launch)
    pl.when(f < last)(halo_right.start)
    pl.when(f > 0)(halo_left.start)
    each_piece(lambda j: take(1, j))
    for copy in own:
        copy.wait()
    pl.when(f > 0)(halo_right.wait_recv)
    pl.when(f < last)(halo_left.wait_recv)
    each_piece(lambda j: pass_on(1, j))

    def between(t):
        pl.when(t < pieces)(lambda: arrive(2, t))

    attend(f * tiles - tiles, pattern_ref, live_ref, q_ref, kvbuf, att, between)

    def core_copy(slot, j):
        return remote(
            coresend.at[slot, :, columns(j)], corebuf.at[slot, :, columns(j)],
            core_send.at[slot, j], core_recv.at[slot, j], to_core,
        )

    def x_copy(j):
        return remote(
            xsend.at[:, columns(j)], xbuf.at[:, columns(j)], x_send.at[j], x_recv.at[j], to_x
        )

    def project(chunk, j, weights):
        slot, parity = chunk // 2, chunk % 2
        cols = columns(j)
        term = jnp.dot(att[...], weights[:, cols], preferred_element_type=jnp.float32)

        @pl.when(parity != core)
        def _():
            coresend[slot, :, cols] = term.astype(jnp.bfloat16)
            core_copy(slot, j).start()

        @pl.when(parity == core)
        def _():
            out_or_send = slot == x
            core_copy(slot, j).wait_recv()
            both = term + corebuf[slot, :, cols].astype(jnp.float32)

            @pl.when(out_or_send)
            def _():
                out_ref[:, cols] = both

            @pl.when(jnp.logical_not(out_or_send))
            def _():
                xsend[:, cols] = both.astype(jnp.bfloat16)
                x_copy(j).start()

    def step(distance, j):
        def one(chunk):
            across(chunk, j, other).wait_recv()
            project(chunk, j, wbuf.at[chunk])

        pl.when(f >= distance)(lambda: one(f - distance))
        pl.when(f + distance <= last)(lambda: one(f + distance))

    each_piece(lambda j: project(f, j, w_ref))
    each_piece(lambda j: step(1, j))

    def events(j):
        arrive(3, j)
        step(2, j)
        pl.when(j >= 2)(lambda: step(3, j - 2))

    each_piece(events)
    each_piece(lambda j: step(3, j), pieces - 2)

    def finish(j):
        x_copy(j).wait_recv()
        cols = columns(j)
        out_ref[:, cols] = out_ref[:, cols] + xbuf[:, cols].astype(jnp.float32)

    each_piece(finish)

    pl.when(f < last)(halo_right.wait_send)
    pl.when(f > 0)(halo_left.wait_send)

    def drain(j):
        x_copy(j).wait_send()
        for slot in range(2):
            core_copy(slot, j).wait_send()
        pl.when(f < last)(along(f, j, to_right, right_send, True).wait_send)
        pl.when(f > 0)(along(f, j, to_left, left_send, True).wait_send)
        for distance in range(1, frames):

            @pl.when(f >= distance)
            def _():
                chunk = f - distance
                pl.when(f < last)(along(chunk, j, to_right, right_send).wait_send)
                across(chunk, j, mine).wait_send()

            @pl.when(f + distance <= last)
            def _():
                chunk = f + distance
                pl.when(f > 0)(along(chunk, j, to_left, left_send).wait_send)
                across(chunk, j, mine).wait_send()

    each_piece(drain)


def fused_sum(queries, keyvals, out_weight, pattern, live):
    rows, width = queries.shape
    frames = lax.axis_size("frame")
    tiles = pattern.shape[0]
    tile_rows = rows // tiles
    depth, span = out_weight.shape
    pieces = span // COLS
    smem = pl.BlockSpec(memory_space=pltpu.SMEM)
    vmem = pl.BlockSpec(memory_space=pltpu.VMEM)
    anywhere = pl.BlockSpec(memory_space=pl.ANY)
    dma = pltpu.SemaphoreType.DMA
    bf16 = jnp.bfloat16
    return pl.pallas_call(
        functools.partial(fused_kernel, frames),
        out_shape=jax.ShapeDtypeStruct((rows, span), jnp.float32),
        in_specs=[smem, smem, anywhere, anywhere, anywhere],
        out_specs=vmem,
        scratch_shapes=[
            pltpu.VMEM((tiles, tile_rows, width), bf16),
            pltpu.VMEM((2, 3 * tiles, tile_rows, width), bf16),
            pltpu.VMEM((depth, span), bf16),
            pltpu.VMEM((frames, depth, span), bf16),
            pltpu.VMEM((rows, width), bf16),
            pltpu.VMEM((2, rows, span), bf16),
            pltpu.VMEM((2, rows, span), bf16),
            pltpu.VMEM((rows, span), bf16),
            pltpu.VMEM((rows, span), bf16),
            dma((3,)), dma((2,)), dma((2,)),
            dma((frames, pieces)), dma((frames, pieces)), dma((frames, pieces)),
            dma((frames, pieces)), dma((frames, pieces)),
            dma((2, pieces)), dma((2, pieces)), dma((pieces,)), dma((pieces,)),
        ],
        compiler_params=pltpu.CompilerParams(
            collective_id=0, has_side_effects=True, vmem_limit_bytes=FUSED_LIMIT
        ),
        cost_estimate=pl.CostEstimate(
            flops=2 * rows * depth * span * frames, bytes_accessed=8 << 20, transcendentals=1 << 20
        ),
    )(
        pattern,
        live,
        queries.reshape(tiles, tile_rows, width),
        keyvals.reshape(2, tiles, tile_rows, width),
        out_weight,
    )


def per_device(queries, keyvals, residual_in, gate, out_weight, pattern, live):
    size = lax.axis_size
    fits = (
        size("groups") == size("head") == size("sub") == 2
        and size("frame") == 4
        and pattern.shape[0] == TILES_F
        and out_weight.shape[1] <= TILES_F * COLS
        and out_weight.shape[0] % 32 == 0
        and out_weight.shape[1] % COLS == 0
    )
    total = fused_sum if fits else plain_sum
    return residual_in + gate[None, :] * total(queries, keyvals, out_weight, pattern, live)


def solution(mesh):
    in_specs = (
        P(("groups", "frame"), ("head", "sub")),
        P(None, ("groups", "frame"), ("head", "sub")),
        P(("groups", "frame"), ("head", "sub")),
        P(("groups", "head", "sub")),
        P(("head", "sub"), "frame"),
        P(("groups", "frame"), None),
        P(("groups", "frame")),
    )
    out_specs = P(("groups", "frame"), ("head", "sub"))
    return jax.shard_map(
        per_device, mesh=mesh, in_specs=in_specs, out_specs=out_specs, check_vma=False
    )
```

```python
import functools
import math

import jax
import jax.numpy as jnp
from jax import lax
from jax.experimental import pallas as pl
from jax.experimental.pallas import tpu as pltpu
from jax.sharding import PartitionSpec as P

HEAD_DIM = 128
TILES_F = 6
KSEL = 8
COLS = 256
VMEM_LIMIT = 48 * 1024 * 1024
FUSED_LIMIT = 60 * 1024 * 1024
MESH = pl.DeviceIdType.MESH


def padded_2(block, axis, dim, width):
    count = lax.axis_size(axis)
    forward = [(i, i + 1) for i in range(count - 1)]
    backward = [(target, source) for source, target in forward]
    low = lax.ppermute(
        lax.slice_in_dim(block, block.shape[dim] - width, None, axis=dim), axis, forward
    )
    high = lax.ppermute(lax.slice_in_dim(block, 0, width, axis=dim), axis, backward)
    return jnp.concatenate([low, block, high], axis=dim)


def attend(first_tile, pattern_ref, live_ref, q_ref, kv_ref, att_ref, between=None):
    tile_count, tile_rows, width = q_ref.shape
    held = kv_ref.shape[1]
    scale = 1.0 / math.sqrt(HEAD_DIM)
    slot = lax.broadcasted_iota(jnp.int32, (tile_rows, KSEL * tile_rows), 1) // tile_rows

    def one_tile(t, carry):
        ids = [jnp.clip(pattern_ref[t, s] - first_tile, 0, held - 1) for s in range(KSEL)]
        keys = jnp.concatenate([kv_ref[0, i] for i in ids], axis=0)
        values = jnp.concatenate([kv_ref[1, i] for i in ids], axis=0)
        tile_queries = q_ref[t]
        allowed = slot < live_ref[t]
        for h in range(width // HEAD_DIM):
            cols = slice(h * HEAD_DIM, (h + 1) * HEAD_DIM)
            scores = lax.dot_general(
                tile_queries[:, cols],
                keys[:, cols],
                (((1,), (1,)), ((), ())),
                preferred_element_type=jnp.float32,
            )
            scores = jnp.where(allowed, scores * scale, -1e30)
            expo = jnp.exp(scores - jnp.max(scores, axis=-1, keepdims=True))
            probs = expo * (1.0 / jnp.sum(expo, axis=-1, keepdims=True))
            out = jnp.dot(
                probs.astype(jnp.bfloat16), values[:, cols], preferred_element_type=jnp.float32
            )
            rows = pl.ds(pl.multiple_of(t * tile_rows, tile_rows), tile_rows)
            att_ref[rows, cols] = out.astype(jnp.bfloat16)
        if between is not None:
            between(t)
        return carry

    lax.fori_loop(0, tile_count, one_tile, 0)


def attend_kernel(first_ref, pattern_ref, live_ref, q_ref, kv_ref, att_ref):
    attend(first_ref[0], pattern_ref, live_ref, q_ref, kv_ref, att_ref)


def plain_sum(queries, keyvals, out_weight, pattern, live):
    rows, width = queries.shape
    tile_count = pattern.shape[0]
    tile_rows = rows // tile_count
    padded = padded_2(keyvals, "frame", 1, TILES_F * tile_rows)
    first_tile = lax.axis_index("frame") * tile_count - TILES_F
    smem = pl.BlockSpec(memory_space=pltpu.SMEM)
    vmem = pl.BlockSpec(memory_space=pltpu.VMEM)
    attended = pl.pallas_call(
        attend_kernel,
        out_shape=jax.ShapeDtypeStruct((rows, width), jnp.bfloat16),
        in_specs=[smem, smem, smem, vmem, vmem],
        out_specs=vmem,
        compiler_params=pltpu.CompilerParams(vmem_limit_bytes=VMEM_LIMIT),
    )(
        jnp.reshape(first_tile, (1,)).astype(jnp.int32),
        pattern,
        live,
        queries.reshape(tile_count, tile_rows, width),
        padded.reshape(2, -1, tile_rows, width),
    )
    partial_rows = jnp.dot(
        attended,
        lax.all_gather(out_weight, "frame", axis=1, tiled=True),
        preferred_element_type=jnp.float32,
    )
    return lax.psum_scatter(
        partial_rows.astype(jnp.bfloat16), ("head", "sub"), scatter_dimension=1, tiled=True
    ).astype(jnp.float32)


def fused_kernel(
    frames, pattern_ref, live_ref, gate_ref, q_hbm, kv_hbm, w_hbm, res_hbm, out_hbm,
    res_ref, acc_ref, q_ref, kvbuf, w_ref, wbuf, att, coresend, corebuf, xsend, xbuf,
    own_sem, halo_send, halo_recv, right_send, left_send, w_recv, y_send, y_recv,
    core_send, core_recv, x_send, x_recv, out_sem,
):
    g, f = lax.axis_index("groups"), lax.axis_index("frame")
    x, core = lax.axis_index("head"), lax.axis_index("sub")
    tiles = q_ref.shape[0]
    depth, span = w_ref.shape
    pieces = span // COLS
    half = depth // 2
    last = frames - 1
    to_left, to_right = {"frame": f - 1}, {"frame": f + 1}
    to_y, to_core, to_x = {"groups": 1 - g}, {"sub": 1 - core}, {"head": 1 - x}
    mine = pl.ds(pl.multiple_of(g * half, half), half)
    other = pl.ds(pl.multiple_of((1 - g) * half, half), half)

    own = [
        pltpu.make_async_copy(kv_hbm, kvbuf.at[:, pl.ds(tiles, tiles)], own_sem.at[0]),
        pltpu.make_async_copy(q_hbm, q_ref, own_sem.at[1]),
        pltpu.make_async_copy(w_hbm, w_ref, own_sem.at[2]),
        pltpu.make_async_copy(res_hbm, res_ref, own_sem.at[3]),
    ]
    for copy in own:
        copy.start()

    barrier = pltpu.get_barrier_semaphore()

    def greet(where):
        pl.semaphore_signal(barrier, inc=1, device_id=where, device_id_type=MESH)

    for where in (to_y, to_core, to_x):
        greet(where)
    pl.when(f > 0)(lambda: greet(to_left))
    pl.when(f < last)(lambda: greet(to_right))
    ends = jnp.where(f > 0, 1, 0) + jnp.where(f < last, 1, 0)
    pl.semaphore_wait(barrier, 3 + ends)

    def remote(src, dst, send, recv, where):
        return pltpu.make_async_remote_copy(
            src_ref=src, dst_ref=dst, send_sem=send, recv_sem=recv,
            device_id=where, device_id_type=MESH,
        )

    def columns(j):
        return pl.ds(pl.multiple_of(j * COLS, COLS), COLS)

    low, high = kvbuf.at[:, pl.ds(0, tiles)], kvbuf.at[:, pl.ds(2 * tiles, tiles)]
    halo_right = remote(kv_hbm, low, halo_send.at[0], halo_recv.at[0], to_right)
    halo_left = remote(kv_hbm, high, halo_send.at[1], halo_recv.at[1], to_left)

    def along(chunk, j, where, sems, first=False):
        piece = wbuf.at[chunk, mine, columns(j)]
        src = w_hbm.at[mine, columns(j)] if first else piece
        return remote(src, piece, sems.at[chunk, j], w_recv.at[chunk, j], where)

    def across(chunk, j, rows):
        piece = wbuf.at[chunk, rows, columns(j)]
        return remote(piece, piece, y_send.at[chunk, j], y_recv.at[chunk, j], to_y)

    def each_piece(body, start=0):
        def run(j, carry):
            body(j)
            return carry

        lax.fori_loop(start, pieces, run, 0)

    def launch(j):
        pl.when(f < last)(along(f, j, to_right, right_send, True).start)
        pl.when(f > 0)(along(f, j, to_left, left_send, True).start)

    def arrive(distance, j):
        @pl.when(f >= distance)
        def _():
            chunk = f - distance
            along(chunk, j, to_right, right_send).wait_recv()
            pl.when(f < last)(along(chunk, j, to_right, right_send).start)
            across(chunk, j, mine).start()

        @pl.when(f + distance <= last)
        def _():
            chunk = f + distance
            along(chunk, j, to_left, left_send).wait_recv()
            pl.when(f > 0)(along(chunk, j, to_left, left_send).start)
            across(chunk, j, mine).start()

    pl.when(f < last)(halo_right.start)
    pl.when(f > 0)(halo_left.start)
    launch(0)
    for copy in own:
        copy.wait()
    pl.when(f > 0)(halo_right.wait_recv)
    pl.when(f < last)(halo_left.wait_recv)
    each_piece(launch, 1)

    def between(t):
        pl.when(t < pieces)(lambda: arrive(1, t))

    attend(f * tiles - tiles, pattern_ref, live_ref, q_ref, kvbuf, att, between)

    def core_copy(slot, j):
        return remote(
            coresend.at[slot, :, columns(j)], corebuf.at[slot, :, columns(j)],
            core_send.at[slot, j], core_recv.at[slot, j], to_core,
        )

    def x_copy(j):
        return remote(
            xsend.at[:, columns(j)], xbuf.at[:, columns(j)], x_send.at[j], x_recv.at[j], to_x
        )

    def project(chunk, j, weights):
        slot, parity = chunk // 2, chunk % 2
        cols = columns(j)
        term = jnp.dot(att[...], weights[:, cols], preferred_element_type=jnp.float32)

        @pl.when(parity != core)
        def _():
            coresend[slot, :, cols] = term.astype(jnp.bfloat16)
            core_copy(slot, j).start()

        @pl.when(parity == core)
        def _():
            out_or_send = slot == x
            core_copy(slot, j).wait_recv()
            both = term + corebuf[slot, :, cols].astype(jnp.float32)

            @pl.when(out_or_send)
            def _():
                acc_ref[:, cols] = both

            @pl.when(jnp.logical_not(out_or_send))
            def _():
                xsend[:, cols] = both.astype(jnp.bfloat16)
                x_copy(j).start()

    def step(distance, j):
        def one(chunk):
            across(chunk, j, other).wait_recv()
            project(chunk, j, wbuf.at[chunk])

        pl.when(f >= distance)(lambda: one(f - distance))
        pl.when(f + distance <= last)(lambda: one(f + distance))

    each_piece(lambda j: project(f, j, w_ref))
    for distance in range(1, last):

        def events(j):
            arrive(distance + 1, j)
            step(distance, j)
            if distance + 1 == last:
                pl.when(j >= 2)(lambda: step(last, j - 2))

        each_piece(events)
    each_piece(lambda j: step(last, j), pieces - 2)

    def out_copy(j):
        cols = columns(j)
        return pltpu.make_async_copy(acc_ref.at[:, cols], out_hbm.at[:, cols], out_sem.at[j])

    def finish(j):
        x_copy(j).wait_recv()
        cols = columns(j)
        summed = acc_ref[:, cols] + xbuf[:, cols].astype(jnp.float32)
        acc_ref[:, cols] = res_ref[:, cols] + gate_ref[:, cols] * summed
        out_copy(j).start()

    each_piece(finish)

    pl.when(f < last)(halo_right.wait_send)
    pl.when(f > 0)(halo_left.wait_send)

    def drain(j):
        out_copy(j).wait()
        x_copy(j).wait_send()
        for slot in range(2):
            core_copy(slot, j).wait_send()
        pl.when(f < last)(along(f, j, to_right, right_send, True).wait_send)
        pl.when(f > 0)(along(f, j, to_left, left_send, True).wait_send)
        for distance in range(1, frames):

            @pl.when(f >= distance)
            def _():
                chunk = f - distance
                pl.when(f < last)(along(chunk, j, to_right, right_send).wait_send)
                across(chunk, j, mine).wait_send()

            @pl.when(f + distance <= last)
            def _():
                chunk = f + distance
                pl.when(f > 0)(along(chunk, j, to_left, left_send).wait_send)
                across(chunk, j, mine).wait_send()

    each_piece(drain)


def fused(queries, keyvals, residual_in, gate, out_weight, pattern, live):
    rows, width = queries.shape
    frames = lax.axis_size("frame")
    tiles = pattern.shape[0]
    tile_rows = rows // tiles
    depth, span = out_weight.shape
    pieces = span // COLS
    smem = pl.BlockSpec(memory_space=pltpu.SMEM)
    vmem = pl.BlockSpec(memory_space=pltpu.VMEM)
    anywhere = pl.BlockSpec(memory_space=pl.ANY)
    dma = pltpu.SemaphoreType.DMA
    bf16 = jnp.bfloat16
    return pl.pallas_call(
        functools.partial(fused_kernel, frames),
        out_shape=jax.ShapeDtypeStruct((rows, span), jnp.float32),
        in_specs=[smem, smem, vmem, anywhere, anywhere, anywhere, anywhere],
        out_specs=anywhere,
        scratch_shapes=[
            pltpu.VMEM((rows, span), jnp.float32),
            pltpu.VMEM((rows, span), jnp.float32),
            pltpu.VMEM((tiles, tile_rows, width), bf16),
            pltpu.VMEM((2, 3 * tiles, tile_rows, width), bf16),
            pltpu.VMEM((depth, span), bf16),
            pltpu.VMEM((frames, depth, span), bf16),
            pltpu.VMEM((rows, width), bf16),
            pltpu.VMEM((2, rows, span), bf16),
            pltpu.VMEM((2, rows, span), bf16),
            pltpu.VMEM((rows, span), bf16),
            pltpu.VMEM((rows, span), bf16),
            dma((4,)), dma((2,)), dma((2,)),
            dma((frames, pieces)), dma((frames, pieces)), dma((frames, pieces)),
            dma((frames, pieces)), dma((frames, pieces)),
            dma((2, pieces)), dma((2, pieces)), dma((pieces,)), dma((pieces,)),
            dma((pieces,)),
        ],
        compiler_params=pltpu.CompilerParams(
            collective_id=0, has_side_effects=True, vmem_limit_bytes=FUSED_LIMIT
        ),
        cost_estimate=pl.CostEstimate(
            flops=2 * rows * depth * span * frames, bytes_accessed=8 << 20, transcendentals=1 << 20
        ),
    )(
        pattern,
        live,
        gate.reshape(1, span),
        queries.reshape(tiles, tile_rows, width),
        keyvals.reshape(2, tiles, tile_rows, width),
        out_weight,
        residual_in,
    )


def per_device(queries, keyvals, residual_in, gate, out_weight, pattern, live):
    size = lax.axis_size
    fits = (
        size("groups") == size("head") == size("sub") == 2
        and size("frame") == 4
        and pattern.shape[0] == TILES_F
        and out_weight.shape[1] <= TILES_F * COLS
        and out_weight.shape[0] % 32 == 0
        and out_weight.shape[1] % COLS == 0
    )
    if fits:
        return fused(queries, keyvals, residual_in, gate, out_weight, pattern, live)
    summed = plain_sum(queries, keyvals, out_weight, pattern, live)
    return residual_in + gate[None, :] * summed


def solution(mesh):
    in_specs = (
        P(("groups", "frame"), ("head", "sub")),
        P(None, ("groups", "frame"), ("head", "sub")),
        P(("groups", "frame"), ("head", "sub")),
        P(("groups", "head", "sub")),
        P(("head", "sub"), "frame"),
        P(("groups", "frame"), None),
        P(("groups", "frame")),
    )
    out_specs = P(("groups", "frame"), ("head", "sub"))
    return jax.shard_map(
        per_device, mesh=mesh, in_specs=in_specs, out_specs=out_specs, check_vma=False
    )
```

```python
import functools
import math

import jax
import jax.numpy as jnp
from jax import lax
from jax.experimental import pallas as pl
from jax.experimental.pallas import tpu as pltpu
from jax.sharding import PartitionSpec as P

HEAD_DIM = 128
TILES_F = 6
KSEL = 8
COLS = 128
LAG = 3
VMEM_LIMIT = 48 * 1024 * 1024
FUSED_LIMIT = 60 * 1024 * 1024
MESH = pl.DeviceIdType.MESH


def padded_2(block, axis, dim, width):
    count = lax.axis_size(axis)
    forward = [(i, i + 1) for i in range(count - 1)]
    backward = [(target, source) for source, target in forward]
    low = lax.ppermute(
        lax.slice_in_dim(block, block.shape[dim] - width, None, axis=dim), axis, forward
    )
    high = lax.ppermute(lax.slice_in_dim(block, 0, width, axis=dim), axis, backward)
    return jnp.concatenate([low, block, high], axis=dim)


def attend(first_tile, pattern_ref, live_ref, q_ref, kv_ref, att_ref, between=None):
    tile_count, tile_rows, width = q_ref.shape
    held = kv_ref.shape[1]
    scale = 1.0 / math.sqrt(HEAD_DIM)
    slot = lax.broadcasted_iota(jnp.int32, (tile_rows, KSEL * tile_rows), 1) // tile_rows

    def one_tile(t, carry):
        ids = [jnp.clip(pattern_ref[t, s] - first_tile, 0, held - 1) for s in range(KSEL)]
        keys = jnp.concatenate([kv_ref[0, i] for i in ids], axis=0)
        values = jnp.concatenate([kv_ref[1, i] for i in ids], axis=0)
        tile_queries = q_ref[t]
        allowed = slot < live_ref[t]
        for h in range(width // HEAD_DIM):
            cols = slice(h * HEAD_DIM, (h + 1) * HEAD_DIM)
            scores = lax.dot_general(
                tile_queries[:, cols],
                keys[:, cols],
                (((1,), (1,)), ((), ())),
                preferred_element_type=jnp.float32,
            )
            scores = jnp.where(allowed, scores * scale, -1e30)
            expo = jnp.exp(scores - jnp.max(scores, axis=-1, keepdims=True))
            probs = expo * (1.0 / jnp.sum(expo, axis=-1, keepdims=True))
            out = jnp.dot(
                probs.astype(jnp.bfloat16), values[:, cols], preferred_element_type=jnp.float32
            )
            rows = pl.ds(pl.multiple_of(t * tile_rows, tile_rows), tile_rows)
            att_ref[rows, cols] = out.astype(jnp.bfloat16)
        if between is not None:
            between(t)
        return carry

    lax.fori_loop(0, tile_count, one_tile, 0)


def attend_kernel(first_ref, pattern_ref, live_ref, q_ref, kv_ref, att_ref):
    attend(first_ref[0], pattern_ref, live_ref, q_ref, kv_ref, att_ref)


def plain_sum(queries, keyvals, out_weight, pattern, live):
    rows, width = queries.shape
    tile_count = pattern.shape[0]
    tile_rows = rows // tile_count
    padded = padded_2(keyvals, "frame", 1, TILES_F * tile_rows)
    first_tile = lax.axis_index("frame") * tile_count - TILES_F
    smem = pl.BlockSpec(memory_space=pltpu.SMEM)
    vmem = pl.BlockSpec(memory_space=pltpu.VMEM)
    attended = pl.pallas_call(
        attend_kernel,
        out_shape=jax.ShapeDtypeStruct((rows, width), jnp.bfloat16),
        in_specs=[smem, smem, smem, vmem, vmem],
        out_specs=vmem,
        compiler_params=pltpu.CompilerParams(vmem_limit_bytes=VMEM_LIMIT),
    )(
        jnp.reshape(first_tile, (1,)).astype(jnp.int32),
        pattern,
        live,
        queries.reshape(tile_count, tile_rows, width),
        padded.reshape(2, -1, tile_rows, width),
    )
    partial_rows = jnp.dot(
        attended,
        lax.all_gather(out_weight, "frame", axis=1, tiled=True),
        preferred_element_type=jnp.float32,
    )
    return lax.psum_scatter(
        partial_rows.astype(jnp.bfloat16), ("head", "sub"), scatter_dimension=1, tiled=True
    ).astype(jnp.float32)


def fused_kernel(
    frames, pattern_ref, live_ref, q_hbm, kv_hbm, w_hbm, out_ref,
    q_ref, kvbuf, w_ref, wbuf, att, coresend, corebuf, xsend, xbuf,
    own_sem, halo_send, halo_recv, right_send, left_send, w_recv, y_send, y_recv,
    core_send, core_recv, x_send, x_recv,
):
    g, f = lax.axis_index("groups"), lax.axis_index("frame")
    x, core = lax.axis_index("head"), lax.axis_index("sub")
    tiles = q_ref.shape[0]
    depth, span = w_ref.shape
    pieces = span // COLS
    half = depth // 2
    last = frames - 1
    to_left, to_right = {"frame": f - 1}, {"frame": f + 1}
    to_y, to_core, to_x = {"groups": 1 - g}, {"sub": 1 - core}, {"head": 1 - x}
    mine = pl.ds(pl.multiple_of(g * half, half), half)
    other = pl.ds(pl.multiple_of((1 - g) * half, half), half)

    own = [
        pltpu.make_async_copy(kv_hbm, kvbuf.at[:, pl.ds(tiles, tiles)], own_sem.at[0]),
        pltpu.make_async_copy(q_hbm, q_ref, own_sem.at[1]),
        pltpu.make_async_copy(w_hbm, w_ref, own_sem.at[2]),
    ]
    for copy in own:
        copy.start()

    barrier = pltpu.get_barrier_semaphore()

    def greet(where):
        pl.semaphore_signal(barrier, inc=1, device_id=where, device_id_type=MESH)

    for where in (to_y, to_core, to_x):
        greet(where)
    pl.when(f > 0)(lambda: greet(to_left))
    pl.when(f < last)(lambda: greet(to_right))
    ends = jnp.where(f > 0, 1, 0) + jnp.where(f < last, 1, 0)
    pl.semaphore_wait(barrier, 3 + ends)

    def remote(src, dst, send, recv, where):
        return pltpu.make_async_remote_copy(
            src_ref=src, dst_ref=dst, send_sem=send, recv_sem=recv,
            device_id=where, device_id_type=MESH,
        )

    def columns(j):
        return pl.ds(pl.multiple_of(j * COLS, COLS), COLS)

    low, high = kvbuf.at[:, pl.ds(0, tiles)], kvbuf.at[:, pl.ds(2 * tiles, tiles)]
    halo_right = remote(kv_hbm, low, halo_send.at[0], halo_recv.at[0], to_right)
    halo_left = remote(kv_hbm, high, halo_send.at[1], halo_recv.at[1], to_left)

    def along(chunk, j, where, sems, first=False):
        piece = wbuf.at[chunk, mine, columns(j)]
        src = w_hbm.at[mine, columns(j)] if first else piece
        return remote(src, piece, sems.at[chunk, j], w_recv.at[chunk, j], where)

    def across(chunk, j, rows):
        piece = wbuf.at[chunk, rows, columns(j)]
        return remote(piece, piece, y_send.at[chunk, j], y_recv.at[chunk, j], to_y)

    def each_piece(body, start=0):
        def run(j, carry):
            body(j)
            return carry

        lax.fori_loop(start, pieces, run, 0)

    def launch(j):
        pl.when(f < last)(along(f, j, to_right, right_send, True).start)
        pl.when(f > 0)(along(f, j, to_left, left_send, True).start)

    def arrive(distance, j):
        @pl.when(f >= distance)
        def _():
            chunk = f - distance
            along(chunk, j, to_right, right_send).wait_recv()
            pl.when(f < last)(along(chunk, j, to_right, right_send).start)
            across(chunk, j, mine).start()

        @pl.when(f + distance <= last)
        def _():
            chunk = f + distance
            along(chunk, j, to_left, left_send).wait_recv()
            pl.when(f > 0)(along(chunk, j, to_left, left_send).start)
            across(chunk, j, mine).start()

    pl.when(f < last)(halo_right.start)
    pl.when(f > 0)(halo_left.start)
    for j in range(2):
        launch(j)
    for copy in own:
        copy.wait()
    pl.when(f > 0)(halo_right.wait_recv)
    pl.when(f < last)(halo_left.wait_recv)
    each_piece(launch, 2)

    def between(t):
        for j in (2 * t, 2 * t + 1):
            pl.when(j < pieces)(functools.partial(arrive, 1, j))

    attend(f * tiles - tiles, pattern_ref, live_ref, q_ref, kvbuf, att, between)

    def core_copy(slot, j):
        return remote(
            coresend.at[slot, :, columns(j)], corebuf.at[slot, :, columns(j)],
            core_send.at[slot, j], core_recv.at[slot, j], to_core,
        )

    def x_copy(j):
        return remote(
            xsend.at[:, columns(j)], xbuf.at[:, columns(j)], x_send.at[j], x_recv.at[j], to_x
        )

    def project(chunk, j, weights):
        slot, parity = chunk // 2, chunk % 2
        cols = columns(j)
        term = jnp.dot(att[...], weights[:, cols], preferred_element_type=jnp.float32)

        @pl.when(parity != core)
        def _():
            coresend[slot, :, cols] = term.astype(jnp.bfloat16)
            core_copy(slot, j).start()

        @pl.when(parity == core)
        def _():
            out_or_send = slot == x
            core_copy(slot, j).wait_recv()
            both = term + corebuf[slot, :, cols].astype(jnp.float32)

            @pl.when(out_or_send)
            def _():
                out_ref[:, cols] = both

            @pl.when(jnp.logical_not(out_or_send))
            def _():
                xsend[:, cols] = both.astype(jnp.bfloat16)
                x_copy(j).start()

    def step(distance, j):
        def one(chunk):
            across(chunk, j, other).wait_recv()
            project(chunk, j, wbuf.at[chunk])

        pl.when(f >= distance)(lambda: one(f - distance))
        pl.when(f + distance <= last)(lambda: one(f + distance))

    each_piece(lambda j: project(f, j, w_ref))
    for distance in range(1, last):

        def events(j):
            arrive(distance + 1, j)
            step(distance, j)
            if distance + 1 == last:
                pl.when(j >= LAG)(lambda: step(last, j - LAG))

        each_piece(events)
    each_piece(lambda j: step(last, j), pieces - LAG)

    def finish(j):
        x_copy(j).wait_recv()
        cols = columns(j)
        out_ref[:, cols] = out_ref[:, cols] + xbuf[:, cols].astype(jnp.float32)

    each_piece(finish)

    pl.when(f < last)(halo_right.wait_send)
    pl.when(f > 0)(halo_left.wait_send)

    def drain(j):
        x_copy(j).wait_send()
        for slot in range(2):
            core_copy(slot, j).wait_send()
        pl.when(f < last)(along(f, j, to_right, right_send, True).wait_send)
        pl.when(f > 0)(along(f, j, to_left, left_send, True).wait_send)
        for distance in range(1, frames):

            @pl.when(f >= distance)
            def _():
                chunk = f - distance
                pl.when(f < last)(along(chunk, j, to_right, right_send).wait_send)
                across(chunk, j, mine).wait_send()

            @pl.when(f + distance <= last)
            def _():
                chunk = f + distance
                pl.when(f > 0)(along(chunk, j, to_left, left_send).wait_send)
                across(chunk, j, mine).wait_send()

    each_piece(drain)


def fused_sum(queries, keyvals, out_weight, pattern, live):
    rows, width = queries.shape
    frames = lax.axis_size("frame")
    tiles = pattern.shape[0]
    tile_rows = rows // tiles
    depth, span = out_weight.shape
    pieces = span // COLS
    smem = pl.BlockSpec(memory_space=pltpu.SMEM)
    vmem = pl.BlockSpec(memory_space=pltpu.VMEM)
    anywhere = pl.BlockSpec(memory_space=pl.ANY)
    dma = pltpu.SemaphoreType.DMA
    bf16 = jnp.bfloat16
    return pl.pallas_call(
        functools.partial(fused_kernel, frames),
        out_shape=jax.ShapeDtypeStruct((rows, span), jnp.float32),
        in_specs=[smem, smem, anywhere, anywhere, anywhere],
        out_specs=vmem,
        scratch_shapes=[
            pltpu.VMEM((tiles, tile_rows, width), bf16),
            pltpu.VMEM((2, 3 * tiles, tile_rows, width), bf16),
            pltpu.VMEM((depth, span), bf16),
            pltpu.VMEM((frames, depth, span), bf16),
            pltpu.VMEM((rows, width), bf16),
            pltpu.VMEM((2, rows, span), bf16),
            pltpu.VMEM((2, rows, span), bf16),
            pltpu.VMEM((rows, span), bf16),
            pltpu.VMEM((rows, span), bf16),
            dma((3,)), dma((2,)), dma((2,)),
            dma((frames, pieces)), dma((frames, pieces)), dma((frames, pieces)),
            dma((frames, pieces)), dma((frames, pieces)),
            dma((2, pieces)), dma((2, pieces)), dma((pieces,)), dma((pieces,)),
        ],
        compiler_params=pltpu.CompilerParams(
            collective_id=0, has_side_effects=True, vmem_limit_bytes=FUSED_LIMIT
        ),
        cost_estimate=pl.CostEstimate(
            flops=2 * rows * depth * span * frames, bytes_accessed=8 << 20, transcendentals=1 << 20
        ),
    )(
        pattern,
        live,
        queries.reshape(tiles, tile_rows, width),
        keyvals.reshape(2, tiles, tile_rows, width),
        out_weight,
    )


def per_device(queries, keyvals, residual_in, gate, out_weight, pattern, live):
    size = lax.axis_size
    fits = (
        size("groups") == size("head") == size("sub") == 2
        and size("frame") == 4
        and pattern.shape[0] == TILES_F
        and out_weight.shape[1] <= 2 * TILES_F * COLS
        and out_weight.shape[0] % 32 == 0
        and out_weight.shape[1] % COLS == 0
    )
    total = fused_sum if fits else plain_sum
    return residual_in + gate[None, :] * total(queries, keyvals, out_weight, pattern, live)


def solution(mesh):
    in_specs = (
        P(("groups", "frame"), ("head", "sub")),
        P(None, ("groups", "frame"), ("head", "sub")),
        P(("groups", "frame"), ("head", "sub")),
        P(("groups", "head", "sub")),
        P(("head", "sub"), "frame"),
        P(("groups", "frame"), None),
        P(("groups", "frame")),
    )
    out_specs = P(("groups", "frame"), ("head", "sub"))
    return jax.shard_map(
        per_device, mesh=mesh, in_specs=in_specs, out_specs=out_specs, check_vma=False
    )
```

```python
import functools
import math

import jax
import jax.numpy as jnp
from jax import lax
from jax.experimental import pallas as pl
from jax.experimental.pallas import tpu as pltpu
from jax.sharding import PartitionSpec as P

HEAD_DIM = 128
TILES_F = 6
KSEL = 8
COLS = 256
VMEM_LIMIT = 48 * 1024 * 1024
FUSED_LIMIT = 60 * 1024 * 1024
MESH = pl.DeviceIdType.MESH


def padded_2(block, axis, dim, width):
    count = lax.axis_size(axis)
    forward = [(i, i + 1) for i in range(count - 1)]
    backward = [(target, source) for source, target in forward]
    low = lax.ppermute(
        lax.slice_in_dim(block, block.shape[dim] - width, None, axis=dim), axis, forward
    )
    high = lax.ppermute(lax.slice_in_dim(block, 0, width, axis=dim), axis, backward)
    return jnp.concatenate([low, block, high], axis=dim)


def attend(first_tile, pattern_ref, live_ref, q_ref, kv_ref, att_ref, between=None):
    tile_count, tile_rows, width = q_ref.shape
    held = kv_ref.shape[1]
    scale = 1.0 / math.sqrt(HEAD_DIM)
    slot = lax.broadcasted_iota(jnp.int32, (tile_rows, KSEL * tile_rows), 1) // tile_rows

    def one_tile(t, carry):
        ids = [jnp.clip(pattern_ref[t, s] - first_tile, 0, held - 1) for s in range(KSEL)]
        keys = jnp.concatenate([kv_ref[0, i] for i in ids], axis=0)
        values = jnp.concatenate([kv_ref[1, i] for i in ids], axis=0)
        tile_queries = q_ref[t]
        allowed = slot < live_ref[t]
        for h in range(width // HEAD_DIM):
            cols = slice(h * HEAD_DIM, (h + 1) * HEAD_DIM)
            scores = lax.dot_general(
                tile_queries[:, cols],
                keys[:, cols],
                (((1,), (1,)), ((), ())),
                preferred_element_type=jnp.float32,
            )
            scores = jnp.where(allowed, scores * scale, -1e30)
            expo = jnp.exp(scores - jnp.max(scores, axis=-1, keepdims=True))
            probs = expo * (1.0 / jnp.sum(expo, axis=-1, keepdims=True))
            out = jnp.dot(
                probs.astype(jnp.bfloat16), values[:, cols], preferred_element_type=jnp.float32
            )
            rows = pl.ds(pl.multiple_of(t * tile_rows, tile_rows), tile_rows)
            att_ref[rows, cols] = out.astype(jnp.bfloat16)
        if between is not None:
            between(t)
        return carry

    lax.fori_loop(0, tile_count, one_tile, 0)


def attend_kernel(first_ref, pattern_ref, live_ref, q_ref, kv_ref, att_ref):
    attend(first_ref[0], pattern_ref, live_ref, q_ref, kv_ref, att_ref)


def plain_sum(queries, keyvals, out_weight, pattern, live):
    rows, width = queries.shape
    tile_count = pattern.shape[0]
    tile_rows = rows // tile_count
    padded = padded_2(keyvals, "frame", 1, TILES_F * tile_rows)
    first_tile = lax.axis_index("frame") * tile_count - TILES_F
    smem = pl.BlockSpec(memory_space=pltpu.SMEM)
    vmem = pl.BlockSpec(memory_space=pltpu.VMEM)
    attended = pl.pallas_call(
        attend_kernel,
        out_shape=jax.ShapeDtypeStruct((rows, width), jnp.bfloat16),
        in_specs=[smem, smem, smem, vmem, vmem],
        out_specs=vmem,
        compiler_params=pltpu.CompilerParams(vmem_limit_bytes=VMEM_LIMIT),
    )(
        jnp.reshape(first_tile, (1,)).astype(jnp.int32),
        pattern,
        live,
        queries.reshape(tile_count, tile_rows, width),
        padded.reshape(2, -1, tile_rows, width),
    )
    partial_rows = jnp.dot(
        attended,
        lax.all_gather(out_weight, "frame", axis=1, tiled=True),
        preferred_element_type=jnp.float32,
    )
    return lax.psum_scatter(
        partial_rows.astype(jnp.bfloat16), ("head", "sub"), scatter_dimension=1, tiled=True
    ).astype(jnp.float32)


def fused_kernel(
    frames, pattern_ref, live_ref, q_hbm, kv_hbm, w_hbm, out_hbm,
    acc_ref, q_ref, kvbuf, w_ref, wbuf, att, coresend, corebuf, xsend, xbuf,
    own_sem, halo_send, halo_recv, right_send, left_send, w_recv, y_send, y_recv,
    core_send, core_recv, x_send, x_recv, out_sem,
):
    g, f = lax.axis_index("groups"), lax.axis_index("frame")
    x, core = lax.axis_index("head"), lax.axis_index("sub")
    tiles = q_ref.shape[0]
    depth, span = w_ref.shape
    pieces = span // COLS
    half = depth // 2
    last = frames - 1
    to_left, to_right = {"frame": f - 1}, {"frame": f + 1}
    to_y, to_core, to_x = {"groups": 1 - g}, {"sub": 1 - core}, {"head": 1 - x}
    mine = pl.ds(pl.multiple_of(g * half, half), half)
    other = pl.ds(pl.multiple_of((1 - g) * half, half), half)

    own = [
        pltpu.make_async_copy(kv_hbm, kvbuf.at[:, pl.ds(tiles, tiles)], own_sem.at[0]),
        pltpu.make_async_copy(q_hbm, q_ref, own_sem.at[1]),
        pltpu.make_async_copy(w_hbm, w_ref, own_sem.at[2]),
    ]
    for copy in reversed(own):
        copy.start()

    barrier = pltpu.get_barrier_semaphore()

    def greet(where):
        pl.semaphore_signal(barrier, inc=1, device_id=where, device_id_type=MESH)

    for where in (to_y, to_core, to_x):
        greet(where)
    pl.when(f > 0)(lambda: greet(to_left))
    pl.when(f < last)(lambda: greet(to_right))
    ends = jnp.where(f > 0, 1, 0) + jnp.where(f < last, 1, 0)
    pl.semaphore_wait(barrier, 3 + ends)

    def remote(src, dst, send, recv, where):
        return pltpu.make_async_remote_copy(
            src_ref=src, dst_ref=dst, send_sem=send, recv_sem=recv,
            device_id=where, device_id_type=MESH,
        )

    def columns(j):
        return pl.ds(pl.multiple_of(j * COLS, COLS), COLS)

    low, high = kvbuf.at[:, pl.ds(0, tiles)], kvbuf.at[:, pl.ds(2 * tiles, tiles)]
    halo_right = remote(kv_hbm, low, halo_send.at[0], halo_recv.at[0], to_right)
    halo_left = remote(kv_hbm, high, halo_send.at[1], halo_recv.at[1], to_left)

    def along(chunk, j, where, sems, first=False):
        piece = wbuf.at[chunk, mine, columns(j)]
        src = w_ref.at[mine, columns(j)] if first else piece
        return remote(src, piece, sems.at[chunk, j], w_recv.at[chunk, j], where)

    def across(chunk, j, rows):
        piece = wbuf.at[chunk, rows, columns(j)]
        return remote(piece, piece, y_send.at[chunk, j], y_recv.at[chunk, j], to_y)

    def each_piece(body, start=0):
        def run(j, carry):
            body(j)
            return carry

        lax.fori_loop(start, pieces, run, 0)

    def launch(j):
        pl.when(f < last)(along(f, j, to_right, right_send, True).start)
        pl.when(f > 0)(along(f, j, to_left, left_send, True).start)

    def arrive(distance, j):
        @pl.when(f >= distance)
        def _():
            chunk = f - distance
            along(chunk, j, to_right, right_send).wait_recv()
            pl.when(f < last)(along(chunk, j, to_right, right_send).start)
            across(chunk, j, mine).start()

        @pl.when(f + distance <= last)
        def _():
            chunk = f + distance
            along(chunk, j, to_left, left_send).wait_recv()
            pl.when(f > 0)(along(chunk, j, to_left, left_send).start)
            across(chunk, j, mine).start()

    pl.when(f < last)(halo_right.start)
    pl.when(f > 0)(halo_left.start)
    own[2].wait()
    launch(0)
    for copy in own[:2]:
        copy.wait()
    pl.when(f > 0)(halo_right.wait_recv)
    pl.when(f < last)(halo_left.wait_recv)
    each_piece(launch, 1)

    def between(t):
        pl.when(t < pieces)(lambda: arrive(1, t))

    attend(f * tiles - tiles, pattern_ref, live_ref, q_ref, kvbuf, att, between)

    def core_copy(slot, j):
        return remote(
            coresend.at[slot, :, columns(j)], corebuf.at[slot, :, columns(j)],
            core_send.at[slot, j], core_recv.at[slot, j], to_core,
        )

    def x_copy(j):
        return remote(
            xsend.at[:, columns(j)], xbuf.at[:, columns(j)], x_send.at[j], x_recv.at[j], to_x
        )

    def project(chunk, j, weights):
        slot, parity = chunk // 2, chunk % 2
        cols = columns(j)
        term = jnp.dot(att[...], weights[:, cols], preferred_element_type=jnp.float32)

        @pl.when(parity != core)
        def _():
            coresend[slot, :, cols] = term.astype(jnp.bfloat16)
            core_copy(slot, j).start()

        @pl.when(parity == core)
        def _():
            out_or_send = slot == x
            core_copy(slot, j).wait_recv()
            both = term + corebuf[slot, :, cols].astype(jnp.float32)

            @pl.when(out_or_send)
            def _():
                acc_ref[:, cols] = both

            @pl.when(jnp.logical_not(out_or_send))
            def _():
                xsend[:, cols] = both.astype(jnp.bfloat16)
                x_copy(j).start()

    def step(distance, j):
        def one(chunk):
            across(chunk, j, other).wait_recv()
            project(chunk, j, wbuf.at[chunk])

        pl.when(f >= distance)(lambda: one(f - distance))
        pl.when(f + distance <= last)(lambda: one(f + distance))

    each_piece(lambda j: project(f, j, w_ref))
    for distance in range(1, last):

        def events(j):
            arrive(distance + 1, j)
            step(distance, j)
            if distance + 1 == last:
                pl.when(j >= 2)(lambda: step(last, j - 2))

        each_piece(events)
    each_piece(lambda j: step(last, j), pieces - 2)

    def out_copy(j):
        cols = columns(j)
        return pltpu.make_async_copy(acc_ref.at[:, cols], out_hbm.at[:, cols], out_sem.at[j])

    def finish(j):
        x_copy(j).wait_recv()
        cols = columns(j)
        acc_ref[:, cols] = acc_ref[:, cols] + xbuf[:, cols].astype(jnp.float32)
        out_copy(j).start()

    each_piece(finish)

    pl.when(f < last)(halo_right.wait_send)
    pl.when(f > 0)(halo_left.wait_send)

    def drain(j):
        out_copy(j).wait()
        x_copy(j).wait_send()
        for slot in range(2):
            core_copy(slot, j).wait_send()
        pl.when(f < last)(along(f, j, to_right, right_send, True).wait_send)
        pl.when(f > 0)(along(f, j, to_left, left_send, True).wait_send)
        for distance in range(1, frames):

            @pl.when(f >= distance)
            def _():
                chunk = f - distance
                pl.when(f < last)(along(chunk, j, to_right, right_send).wait_send)
                across(chunk, j, mine).wait_send()

            @pl.when(f + distance <= last)
            def _():
                chunk = f + distance
                pl.when(f > 0)(along(chunk, j, to_left, left_send).wait_send)
                across(chunk, j, mine).wait_send()

    each_piece(drain)


def fused_sum(queries, keyvals, out_weight, pattern, live):
    rows, width = queries.shape
    frames = lax.axis_size("frame")
    tiles = pattern.shape[0]
    tile_rows = rows // tiles
    depth, span = out_weight.shape
    pieces = span // COLS
    smem = pl.BlockSpec(memory_space=pltpu.SMEM)
    anywhere = pl.BlockSpec(memory_space=pl.ANY)
    dma = pltpu.SemaphoreType.DMA
    bf16 = jnp.bfloat16
    return pl.pallas_call(
        functools.partial(fused_kernel, frames),
        out_shape=jax.ShapeDtypeStruct((rows, span), jnp.float32),
        in_specs=[smem, smem, anywhere, anywhere, anywhere],
        out_specs=anywhere,
        scratch_shapes=[
            pltpu.VMEM((rows, span), jnp.float32),
            pltpu.VMEM((tiles, tile_rows, width), bf16),
            pltpu.VMEM((2, 3 * tiles, tile_rows, width), bf16),
            pltpu.VMEM((depth, span), bf16),
            pltpu.VMEM((frames, depth, span), bf16),
            pltpu.VMEM((rows, width), bf16),
            pltpu.VMEM((2, rows, span), bf16),
            pltpu.VMEM((2, rows, span), bf16),
            pltpu.VMEM((rows, span), bf16),
            pltpu.VMEM((rows, span), bf16),
            dma((3,)), dma((2,)), dma((2,)),
            dma((frames, pieces)), dma((frames, pieces)), dma((frames, pieces)),
            dma((frames, pieces)), dma((frames, pieces)),
            dma((2, pieces)), dma((2, pieces)), dma((pieces,)), dma((pieces,)),
            dma((pieces,)),
        ],
        compiler_params=pltpu.CompilerParams(
            collective_id=0, has_side_effects=True, vmem_limit_bytes=FUSED_LIMIT
        ),
        cost_estimate=pl.CostEstimate(
            flops=2 * rows * depth * span * frames, bytes_accessed=8 << 20, transcendentals=1 << 20
        ),
    )(
        pattern,
        live,
        queries.reshape(tiles, tile_rows, width),
        keyvals.reshape(2, tiles, tile_rows, width),
        out_weight,
    )


def per_device(queries, keyvals, residual_in, gate, out_weight, pattern, live):
    size = lax.axis_size
    fits = (
        size("groups") == size("head") == size("sub") == 2
        and size("frame") == 4
        and pattern.shape[0] == TILES_F
        and out_weight.shape[1] <= TILES_F * COLS
        and out_weight.shape[0] % 32 == 0
        and out_weight.shape[1] % COLS == 0
    )
    total = fused_sum if fits else plain_sum
    return residual_in + gate[None, :] * total(queries, keyvals, out_weight, pattern, live)


def solution(mesh):
    in_specs = (
        P(("groups", "frame"), ("head", "sub")),
        P(None, ("groups", "frame"), ("head", "sub")),
        P(("groups", "frame"), ("head", "sub")),
        P(("groups", "head", "sub")),
        P(("head", "sub"), "frame"),
        P(("groups", "frame"), None),
        P(("groups", "frame")),
    )
    out_specs = P(("groups", "frame"), ("head", "sub"))
    return jax.shard_map(
        per_device, mesh=mesh, in_specs=in_specs, out_specs=out_specs, check_vma=False
    )
```

```python
import functools
import math

import jax
import jax.numpy as jnp
from jax import lax
from jax.experimental import pallas as pl
from jax.experimental.pallas import tpu as pltpu
from jax.sharding import PartitionSpec as P

HEAD_DIM = 128
TILES_F = 6
KSEL = 8
COLS = 256
AHEAD = 3
VMEM_LIMIT = 48 * 1024 * 1024
FUSED_LIMIT = 60 * 1024 * 1024
MESH = pl.DeviceIdType.MESH


def padded_2(block, axis, dim, width):
    count = lax.axis_size(axis)
    forward = [(i, i + 1) for i in range(count - 1)]
    backward = [(target, source) for source, target in forward]
    low = lax.ppermute(
        lax.slice_in_dim(block, block.shape[dim] - width, None, axis=dim), axis, forward
    )
    high = lax.ppermute(lax.slice_in_dim(block, 0, width, axis=dim), axis, backward)
    return jnp.concatenate([low, block, high], axis=dim)


def attend(first_tile, pattern_ref, live_ref, q_ref, kv_ref, att_ref, between=None):
    tile_count, tile_rows, width = q_ref.shape
    held = kv_ref.shape[1]
    scale = 1.0 / math.sqrt(HEAD_DIM)
    slot = lax.broadcasted_iota(jnp.int32, (tile_rows, KSEL * tile_rows), 1) // tile_rows

    def one_tile(t, carry):
        ids = [jnp.clip(pattern_ref[t, s] - first_tile, 0, held - 1) for s in range(KSEL)]
        keys = jnp.concatenate([kv_ref[0, i] for i in ids], axis=0)
        values = jnp.concatenate([kv_ref[1, i] for i in ids], axis=0)
        tile_queries = q_ref[t]
        allowed = slot < live_ref[t]
        for h in range(width // HEAD_DIM):
            cols = slice(h * HEAD_DIM, (h + 1) * HEAD_DIM)
            scores = lax.dot_general(
                tile_queries[:, cols],
                keys[:, cols],
                (((1,), (1,)), ((), ())),
                preferred_element_type=jnp.float32,
            )
            scores = jnp.where(allowed, scores * scale, -1e30)
            expo = jnp.exp(scores - jnp.max(scores, axis=-1, keepdims=True))
            probs = expo * (1.0 / jnp.sum(expo, axis=-1, keepdims=True))
            out = jnp.dot(
                probs.astype(jnp.bfloat16), values[:, cols], preferred_element_type=jnp.float32
            )
            rows = pl.ds(pl.multiple_of(t * tile_rows, tile_rows), tile_rows)
            att_ref[rows, cols] = out.astype(jnp.bfloat16)
        if between is not None:
            between(t)
        return carry

    lax.fori_loop(0, tile_count, one_tile, 0)


def attend_kernel(first_ref, pattern_ref, live_ref, q_ref, kv_ref, att_ref):
    attend(first_ref[0], pattern_ref, live_ref, q_ref, kv_ref, att_ref)


def plain_sum(queries, keyvals, out_weight, pattern, live):
    rows, width = queries.shape
    tile_count = pattern.shape[0]
    tile_rows = rows // tile_count
    padded = padded_2(keyvals, "frame", 1, TILES_F * tile_rows)
    first_tile = lax.axis_index("frame") * tile_count - TILES_F
    smem = pl.BlockSpec(memory_space=pltpu.SMEM)
    vmem = pl.BlockSpec(memory_space=pltpu.VMEM)
    attended = pl.pallas_call(
        attend_kernel,
        out_shape=jax.ShapeDtypeStruct((rows, width), jnp.bfloat16),
        in_specs=[smem, smem, smem, vmem, vmem],
        out_specs=vmem,
        compiler_params=pltpu.CompilerParams(vmem_limit_bytes=VMEM_LIMIT),
    )(
        jnp.reshape(first_tile, (1,)).astype(jnp.int32),
        pattern,
        live,
        queries.reshape(tile_count, tile_rows, width),
        padded.reshape(2, -1, tile_rows, width),
    )
    partial_rows = jnp.dot(
        attended,
        lax.all_gather(out_weight, "frame", axis=1, tiled=True),
        preferred_element_type=jnp.float32,
    )
    return lax.psum_scatter(
        partial_rows.astype(jnp.bfloat16), ("head", "sub"), scatter_dimension=1, tiled=True
    ).astype(jnp.float32)


def fused_kernel(
    frames, pattern_ref, live_ref, q_hbm, kv_hbm, w_hbm, out_hbm,
    acc_ref, q_ref, kvbuf, w_ref, wbuf, att, coresend, corebuf, xsend, xbuf,
    own_sem, halo_send, halo_recv, right_send, left_send, w_recv, y_send, y_recv,
    core_send, core_recv, x_send, x_recv, out_sem,
):
    g, f = lax.axis_index("groups"), lax.axis_index("frame")
    x, core = lax.axis_index("head"), lax.axis_index("sub")
    tiles = q_ref.shape[0]
    depth, span = w_ref.shape
    pieces = span // COLS
    half = depth // 2
    last = frames - 1
    to_left, to_right = {"frame": f - 1}, {"frame": f + 1}
    to_y, to_core, to_x = {"groups": 1 - g}, {"sub": 1 - core}, {"head": 1 - x}
    mine = pl.ds(pl.multiple_of(g * half, half), half)
    other = pl.ds(pl.multiple_of((1 - g) * half, half), half)

    own = [
        pltpu.make_async_copy(kv_hbm, kvbuf.at[:, pl.ds(tiles, tiles)], own_sem.at[0]),
        pltpu.make_async_copy(q_hbm, q_ref, own_sem.at[1]),
        pltpu.make_async_copy(w_hbm, w_ref, own_sem.at[2]),
    ]
    for copy in reversed(own):
        copy.start()

    barrier = pltpu.get_barrier_semaphore()

    def greet(where):
        pl.semaphore_signal(barrier, inc=1, device_id=where, device_id_type=MESH)

    for where in (to_y, to_core, to_x):
        greet(where)
    pl.when(f > 0)(lambda: greet(to_left))
    pl.when(f < last)(lambda: greet(to_right))
    ends = jnp.where(f > 0, 1, 0) + jnp.where(f < last, 1, 0)
    pl.semaphore_wait(barrier, 3 + ends)

    def remote(src, dst, send, recv, where):
        return pltpu.make_async_remote_copy(
            src_ref=src, dst_ref=dst, send_sem=send, recv_sem=recv,
            device_id=where, device_id_type=MESH,
        )

    def columns(j):
        return pl.ds(pl.multiple_of(j * COLS, COLS), COLS)

    low, high = kvbuf.at[:, pl.ds(0, tiles)], kvbuf.at[:, pl.ds(2 * tiles, tiles)]
    halo_right = remote(kv_hbm, low, halo_send.at[0], halo_recv.at[0], to_right)
    halo_left = remote(kv_hbm, high, halo_send.at[1], halo_recv.at[1], to_left)

    def along(chunk, j, where, sems, first=False):
        piece = wbuf.at[chunk, mine, columns(j)]
        src = w_ref.at[mine, columns(j)] if first else piece
        return remote(src, piece, sems.at[chunk, j], w_recv.at[chunk, j], where)

    def across(chunk, j, rows):
        piece = wbuf.at[chunk, rows, columns(j)]
        return remote(piece, piece, y_send.at[chunk, j], y_recv.at[chunk, j], to_y)

    def each_piece(body, start=0):
        def run(j, carry):
            body(j)
            return carry

        lax.fori_loop(start, pieces, run, 0)

    def launch(j):
        pl.when(f < last)(along(f, j, to_right, right_send, True).start)
        pl.when(f > 0)(along(f, j, to_left, left_send, True).start)

    def arrive(distance, j):
        @pl.when(f >= distance)
        def _():
            chunk = f - distance
            along(chunk, j, to_right, right_send).wait_recv()
            pl.when(f < last)(along(chunk, j, to_right, right_send).start)
            across(chunk, j, mine).start()

        @pl.when(f + distance <= last)
        def _():
            chunk = f + distance
            along(chunk, j, to_left, left_send).wait_recv()
            pl.when(f > 0)(along(chunk, j, to_left, left_send).start)
            across(chunk, j, mine).start()

    pl.when(f < last)(halo_right.start)
    pl.when(f > 0)(halo_left.start)
    own[2].wait()
    for j in range(AHEAD):
        launch(j)
    for copy in own[:2]:
        copy.wait()
    pl.when(f > 0)(halo_right.wait_recv)
    pl.when(f < last)(halo_left.wait_recv)
    each_piece(launch, AHEAD)

    def between(t):
        pl.when(t < pieces)(lambda: arrive(1, t))

    attend(f * tiles - tiles, pattern_ref, live_ref, q_ref, kvbuf, att, between)

    def core_copy(slot, j):
        return remote(
            coresend.at[slot, :, columns(j)], corebuf.at[slot, :, columns(j)],
            core_send.at[slot, j], core_recv.at[slot, j], to_core,
        )

    def x_copy(j):
        return remote(
            xsend.at[:, columns(j)], xbuf.at[:, columns(j)], x_send.at[j], x_recv.at[j], to_x
        )

    def project(chunk, j, weights):
        slot, parity = chunk // 2, chunk % 2
        cols = columns(j)
        term = jnp.dot(att[...], weights[:, cols], preferred_element_type=jnp.float32)

        @pl.when(parity != core)
        def _():
            coresend[slot, :, cols] = term.astype(jnp.bfloat16)
            core_copy(slot, j).start()

        @pl.when(parity == core)
        def _():
            out_or_send = slot == x
            core_copy(slot, j).wait_recv()
            both = term + corebuf[slot, :, cols].astype(jnp.float32)

            @pl.when(out_or_send)
            def _():
                acc_ref[:, cols] = both

            @pl.when(jnp.logical_not(out_or_send))
            def _():
                xsend[:, cols] = both.astype(jnp.bfloat16)
                x_copy(j).start()

    def step(distance, j):
        def one(chunk):
            across(chunk, j, other).wait_recv()
            project(chunk, j, wbuf.at[chunk])

        pl.when(f >= distance)(lambda: one(f - distance))
        pl.when(f + distance <= last)(lambda: one(f + distance))

    each_piece(lambda j: project(f, j, w_ref))
    for distance in range(1, last):

        def events(j):
            arrive(distance + 1, j)
            step(distance, j)
            if distance + 1 == last:
                pl.when(j >= 2)(lambda: step(last, j - 2))

        each_piece(events)
    each_piece(lambda j: step(last, j), pieces - 2)

    def out_copy(j):
        cols = columns(j)
        return pltpu.make_async_copy(acc_ref.at[:, cols], out_hbm.at[:, cols], out_sem.at[j])

    def finish(j):
        x_copy(j).wait_recv()
        cols = columns(j)
        acc_ref[:, cols] = acc_ref[:, cols] + xbuf[:, cols].astype(jnp.float32)
        out_copy(j).start()

    each_piece(finish)

    pl.when(f < last)(halo_right.wait_send)
    pl.when(f > 0)(halo_left.wait_send)

    def drain(j):
        out_copy(j).wait()
        x_copy(j).wait_send()
        for slot in range(2):
            core_copy(slot, j).wait_send()
        pl.when(f < last)(along(f, j, to_right, right_send, True).wait_send)
        pl.when(f > 0)(along(f, j, to_left, left_send, True).wait_send)
        for distance in range(1, frames):

            @pl.when(f >= distance)
            def _():
                chunk = f - distance
                pl.when(f < last)(along(chunk, j, to_right, right_send).wait_send)
                across(chunk, j, mine).wait_send()

            @pl.when(f + distance <= last)
            def _():
                chunk = f + distance
                pl.when(f > 0)(along(chunk, j, to_left, left_send).wait_send)
                across(chunk, j, mine).wait_send()

    each_piece(drain)


def fused_sum(queries, keyvals, out_weight, pattern, live):
    rows, width = queries.shape
    frames = lax.axis_size("frame")
    tiles = pattern.shape[0]
    tile_rows = rows // tiles
    depth, span = out_weight.shape
    pieces = span // COLS
    smem = pl.BlockSpec(memory_space=pltpu.SMEM)
    anywhere = pl.BlockSpec(memory_space=pl.ANY)
    dma = pltpu.SemaphoreType.DMA
    bf16 = jnp.bfloat16
    return pl.pallas_call(
        functools.partial(fused_kernel, frames),
        out_shape=jax.ShapeDtypeStruct((rows, span), jnp.float32),
        in_specs=[smem, smem, anywhere, anywhere, anywhere],
        out_specs=anywhere,
        scratch_shapes=[
            pltpu.VMEM((rows, span), jnp.float32),
            pltpu.VMEM((tiles, tile_rows, width), bf16),
            pltpu.VMEM((2, 3 * tiles, tile_rows, width), bf16),
            pltpu.VMEM((depth, span), bf16),
            pltpu.VMEM((frames, depth, span), bf16),
            pltpu.VMEM((rows, width), bf16),
            pltpu.VMEM((2, rows, span), bf16),
            pltpu.VMEM((2, rows, span), bf16),
            pltpu.VMEM((rows, span), bf16),
            pltpu.VMEM((rows, span), bf16),
            dma((3,)), dma((2,)), dma((2,)),
            dma((frames, pieces)), dma((frames, pieces)), dma((frames, pieces)),
            dma((frames, pieces)), dma((frames, pieces)),
            dma((2, pieces)), dma((2, pieces)), dma((pieces,)), dma((pieces,)),
            dma((pieces,)),
        ],
        compiler_params=pltpu.CompilerParams(
            collective_id=0, has_side_effects=True, vmem_limit_bytes=FUSED_LIMIT
        ),
        cost_estimate=pl.CostEstimate(
            flops=2 * rows * depth * span * frames, bytes_accessed=8 << 20, transcendentals=1 << 20
        ),
    )(
        pattern,
        live,
        queries.reshape(tiles, tile_rows, width),
        keyvals.reshape(2, tiles, tile_rows, width),
        out_weight,
    )


def per_device(queries, keyvals, residual_in, gate, out_weight, pattern, live):
    size = lax.axis_size
    fits = (
        size("groups") == size("head") == size("sub") == 2
        and size("frame") == 4
        and pattern.shape[0] == TILES_F
        and AHEAD * COLS <= out_weight.shape[1] <= TILES_F * COLS
        and out_weight.shape[0] % 32 == 0
        and out_weight.shape[1] % COLS == 0
    )
    total = fused_sum if fits else plain_sum
    return residual_in + gate[None, :] * total(queries, keyvals, out_weight, pattern, live)


def solution(mesh):
    in_specs = (
        P(("groups", "frame"), ("head", "sub")),
        P(None, ("groups", "frame"), ("head", "sub")),
        P(("groups", "frame"), ("head", "sub")),
        P(("groups", "head", "sub")),
        P(("head", "sub"), "frame"),
        P(("groups", "frame"), None),
        P(("groups", "frame")),
    )
    out_specs = P(("groups", "frame"), ("head", "sub"))
    return jax.shard_map(
        per_device, mesh=mesh, in_specs=in_specs, out_specs=out_specs, check_vma=False
    )
```
